256 devices in a mesh: dp: 8 (over y, core), expert: 32 (over z, x).
Axes of the slice: x: 4, y: 4, z: 8, core: 2. Of those that a mesh axis runs over, the one named last changes fastest.
Arguments:
- tokens: bfloat16 [32768, 2048], P(('dp', 'expert')), may hold values from -6 to 6
- cotangent: bfloat16 [32768, 2048], P(('dp', 'expert')), may hold values from -4 to 4
- expert_ids: int32 [32768, 6], P(('dp', 'expert')), may hold values from 0 to 31, all different within a row; in each aligned block of 128 rows (0 to 127, 128 to 255, ...) at most 26 rows name the same one
- gate_values: float32 [32768, 6], P(('dp', 'expert')), may hold values from 0.05 to 0.45
- saved_pre: bfloat16 [32, 8, 32, 26, 1408], P('expert', 'dp'), may hold values from -6 to 6
- w_gate: bfloat16 [32, 2048, 704], P('expert', 'dp'), may hold values from -0.125 to 0.125
- w_up: bfloat16 [32, 2048, 704], P('expert', 'dp'), may hold values from -0.125 to 0.125
- w_down: bfloat16 [32, 704, 2048], P('expert', None, 'dp'), may hold values from -0.21875 to 0.21875
Outputs:
- grad_tokens: bfloat16 [32768, 2048], P(('dp', 'expert'))
- grad_gate: bfloat16 [32, 2048, 704], P('expert', 'dp')
- grad_up: bfloat16 [32, 2048, 704], P('expert', 'dp')
- grad_down: bfloat16 [32, 704, 2048], P('expert', None, 'dp')
The draws below stay inside these ranges and needn't reach their ends.
Inputs may be any that keep to these rules, and one draw needn't show every extreme that they name: `expert_ids`: each row names 6 different experts; the rows of one device name no expert more than 26 times, a bound that some block reaches.
All inputs are finite; a program needn't handle non-finite values.
Results may differ from the reference program's by a relative error of at most 0.019.
Values may be sent and summed in bfloat16 or wider, within the bound.
A program may use at most 128 MiB of HBM per device.

```python
import math
import jax
import jax.numpy as jnp
import numpy as np
from jax import lax

D = 2048
H = 704
TOP = 6
TOK_DEV = 128
EXPERTS = 32
CAP = 26
TOKENS = 32768
N_DP = 8
N_EXPERT = 32


def block_levels(stream_key, extent, shards, smallest, high):
    loudness, own = 1.0, jax.random.fold_in(stream_key, 6)
    for dim, blocks in shards:
        heights = jnp.exp(jax.random.uniform(jax.random.fold_in(own, dim), (blocks,), jnp.float32, smallest / len(shards), high / len(shards)))
        loudness = loudness * jnp.repeat(heights, extent[dim] // blocks).reshape([-1 if axis == dim else 1 for axis in range(len(extent))])
    return loudness


def assign_block(key, own, number, rows, number_of, top, limit, skew):
    order = jax.random.permutation(key, number_of)
    packed, ordinary = shares(number_of, rows * top, limit, skew, True), shares(number_of, rows * top, limit, skew, False)
    places = jnp.arange(number_of)

    def named(tallies, rotation):
        used = int((tallies > 0).sum())
        fixed = max(1, used // 4)
        passed = fixed + (places - fixed + rotation * (used - fixed)) % max(1, number_of - fixed)
        return jnp.zeros((number_of,), jnp.int32).at[order[jnp.where(places < fixed, places, passed)]].set(jnp.asarray(tallies, jnp.int32))

    tallies = jnp.where(number % 4 == 0, named(packed, number // 4), named(ordinary, number - number // 4 - 1))
    mixed = jax.random.permutation(jax.random.fold_in(own, 3), number_of)
    source_of, receiver = mixed[0:number_of // 2 * 2:2], mixed[1:number_of // 2 * 2:2]
    room = jnp.minimum(tallies[source_of] - 1, limit - tallies[receiver]) // 2
    room = jnp.where((source_of == order[0]) | (receiver == order[0]) | (tallies[receiver] == 0), 0, jnp.maximum(room, 0))
    passed = jax.random.randint(jax.random.fold_in(own, 4), (number_of // 2,), 0, 1 << 20) % (room + 1)
    tallies = tallies.at[source_of].add(-passed).at[receiver].add(passed)
    labels = jnp.searchsorted(jnp.cumsum(tallies), jnp.arange(rows * top), side="right").astype(jnp.int32)
    grid = labels.reshape(top, rows).T
    grid = grid[jax.random.permutation(jax.random.fold_in(own, 1), rows)]
    rotation = jax.random.randint(jax.random.fold_in(own, 2), (rows, 1), 0, top)
    return jnp.take_along_axis(grid, (jnp.arange(top)[None, :] + rotation) % top, axis=1)


def shares(count, total, reach, skew, full):
    loads = [(1 << 20) // math.isqrt(rank ** skew) + 1 for rank in range(1, count + 1)]
    largest = reach if full else min(reach, max(-(-total // count), total * loads[0] // sum(loads)))
    least = 1 if total - largest >= count - 1 else 0
    holding, surplus = [largest] + [least] * (count - 1), total - largest - least * (count - 1)
    while surplus > 0:
        movable = [i for i in range(1, count) if holding[i] < largest] or [i for i in range(1, count) if holding[i] < reach]
        mass, left = sum([loads[i] for i in movable]), surplus
        for i in movable:
            addition = min(reach - holding[i], max(1, left * loads[i] // mass), surplus)
            holding[i] = holding[i] + addition
            surplus = surplus - addition
    return np.array(holding)


def scatter_about(key, extent, scale, bound, split=(), kind=jnp.bfloat16):
    array = jax.random.normal(key, extent, jnp.float32) * scale
    if len(split) > 0:
        array = block_levels(key, extent, split, -0.22, 0.18) * array
    return jnp.clip(array, min=-bound, max=bound).astype(kind)


def setup_inputs(seed: int = 0) -> dict:
    key_list = jax.random.split(jax.random.key(seed), 9)
    tokens = scatter_about(key_list[0], (TOKENS, D), 1.0, 6.0, ((0, 256),))
    cotangent = scatter_about(key_list[1], (TOKENS, D), 0.25, 4.0, ((0, 256),))
    expert_ids_keys = jax.random.split(jax.random.fold_in(key_list[2], 1), TOKENS // TOK_DEV)
    expert_ids_turns = jax.random.permutation(jax.random.fold_in(key_list[2], 3), TOKENS // TOK_DEV)
    expert_ids = jax.vmap(lambda own, number: assign_block(jax.random.fold_in(key_list[2], 2), own, number, TOK_DEV, EXPERTS, TOP, CAP, 0))(expert_ids_keys, expert_ids_turns).reshape((TOKENS, TOP))
    gate_values = jnp.clip(0.05 + 0.39999999 * jax.random.uniform(key_list[3], (TOKENS, TOP), jnp.float32) ** block_levels(key_list[3], (TOKENS, TOP), ((0, 256),), -0.2, 0.2), 0.05, 0.45)
    saved_pre = scatter_about(key_list[4], (EXPERTS, N_DP, N_EXPERT, CAP, 2 * H), 1.0, 6.0, ((0, 32), (1, 8)))
    w_gate = scatter_about(key_list[5], (EXPERTS, D, H), D ** -0.5, 0.125, ((0, 32), (1, 8)))
    w_up = scatter_about(key_list[6], (EXPERTS, D, H), D ** -0.5, 0.125, ((0, 32), (1, 8)))
    w_down = scatter_about(key_list[7], (EXPERTS, H, D), H ** -0.5, 0.21875, ((0, 32), (2, 8)))
    return {"tokens": tokens, "cotangent": cotangent, "expert_ids": expert_ids, "gate_values": gate_values, "saved_pre": saved_pre, "w_gate": w_gate, "w_up": w_up, "w_down": w_down}


def block_tables(ids_block, gates_block):
    flat_ids = ids_block.reshape(-1)
    onehot = (flat_ids[:, None] == jnp.arange(EXPERTS, dtype=jnp.int32)[None, :]).astype(jnp.int32)
    before = jnp.cumsum(onehot, axis=0) - onehot
    slot_index = jnp.sum(before * onehot, axis=1).astype(jnp.int32)
    target = (flat_ids * CAP + slot_index).astype(jnp.int32)
    source_row = (jnp.arange(TOK_DEV * TOP, dtype=jnp.int32) // TOP).astype(jnp.int32)
    slot_token = jnp.zeros((EXPERTS * CAP,), jnp.int32).at[target].set(source_row)
    filled = jnp.zeros((EXPERTS * CAP,), jnp.bool_).at[target].set(True)
    slot_gate = jnp.zeros((EXPERTS * CAP,), jnp.float32).at[target].set(gates_block.reshape(-1))
    return slot_token, filled, slot_gate


def reference(tokens, cotangent, expert_ids, gate_values, saved_pre, w_gate, w_up, w_down):
    blocks = N_DP * N_EXPERT
    slot_token, filled, slot_gate = jax.vmap(block_tables)(
        expert_ids.reshape(blocks, TOK_DEV, TOP), gate_values.reshape(blocks, TOK_DEV, TOP))
    offsets = (jnp.arange(blocks, dtype=jnp.int32) * TOK_DEV)[:, None]
    slot_token = (slot_token + offsets).astype(jnp.int32)
    slot_token = jnp.transpose(slot_token.reshape(blocks, EXPERTS, CAP), (1, 0, 2))
    filled = jnp.transpose(filled.reshape(blocks, EXPERTS, CAP), (1, 0, 2))
    slot_gate = jnp.transpose(slot_gate.reshape(blocks, EXPERTS, CAP), (1, 0, 2))

    def one_expert(grad_acc, inputs):
        token_of, fill_of, gate_of, pre_block, gate_w, up_w, down_w = inputs
        index = token_of.reshape(-1)
        slot_rows = jnp.where(fill_of.reshape(-1)[:, None], tokens[index], jnp.zeros((), tokens.dtype))
        slot_grads = (gate_of.reshape(-1)[:, None] * cotangent[index].astype(jnp.float32)).astype(jnp.bfloat16)
        pre_act = pre_block.reshape(-1, 2 * H).astype(jnp.float32)
        pre_gate = pre_act[:, :H]
        pre_up = pre_act[:, H:]
        sigmoid_gate = 1.0 / (1.0 + jnp.exp(-pre_gate))
        hidden_act = (pre_gate * sigmoid_gate * pre_up).astype(jnp.bfloat16)
        grad_hidden = jnp.dot(slot_grads, down_w.T, preferred_element_type=jnp.float32)
        grad_gate_pre = (grad_hidden * pre_up * sigmoid_gate * (1.0 + pre_gate * (1.0 - sigmoid_gate))).astype(jnp.bfloat16)
        grad_up_pre = (grad_hidden * pre_gate * sigmoid_gate).astype(jnp.bfloat16)
        slot_back = (jnp.dot(grad_gate_pre, gate_w.T, preferred_element_type=jnp.float32)
                     + jnp.dot(grad_up_pre, up_w.T, preferred_element_type=jnp.float32)).astype(jnp.bfloat16)
        grad_acc = grad_acc.at[index].add(slot_back.astype(jnp.float32))
        rows_f = slot_rows.astype(jnp.float32).reshape(N_DP, N_EXPERT * CAP, D)
        grads_f = slot_grads.astype(jnp.float32).reshape(N_DP, N_EXPERT * CAP, D)
        gate_pre_f = grad_gate_pre.astype(jnp.float32).reshape(N_DP, N_EXPERT * CAP, H)
        up_pre_f = grad_up_pre.astype(jnp.float32).reshape(N_DP, N_EXPERT * CAP, H)
        hidden_f = hidden_act.astype(jnp.float32).reshape(N_DP, N_EXPERT * CAP, H)
        partial_gate = jnp.einsum("rsd,rsh->rdh", rows_f, gate_pre_f).astype(jnp.bfloat16)
        partial_up = jnp.einsum("rsd,rsh->rdh", rows_f, up_pre_f).astype(jnp.bfloat16)
        partial_down = jnp.einsum("rsh,rsd->rhd", hidden_f, grads_f).astype(jnp.bfloat16)
        grad_g = jnp.sum(partial_gate.astype(jnp.float32), axis=0).astype(jnp.bfloat16)
        grad_u = jnp.sum(partial_up.astype(jnp.float32), axis=0).astype(jnp.bfloat16)
        grad_d = jnp.sum(partial_down.astype(jnp.float32), axis=0).astype(jnp.bfloat16)
        return grad_acc, (grad_g, grad_u, grad_d)

    start_acc = jnp.zeros((TOKENS, D), jnp.float32)
    grad_acc, stacked = lax.scan(one_expert, start_acc,
                                 (slot_token, filled, slot_gate, saved_pre, w_gate, w_up, w_down))
    grad_tokens = grad_acc.astype(jnp.bfloat16)
    return grad_tokens, stacked[0], stacked[1], stacked[2]
```

```python
import jax
import jax.numpy as jnp
from jax import lax
from jax.experimental import pallas as pl
from jax.experimental.pallas import tpu as pltpu
from jax.sharding import PartitionSpec as P

MESH = pl.DeviceIdType.MESH
NZ, NX = 8, 4
CAP = 26
BLK = 128
GRP = NZ * CAP
SLOTS = NX * GRP
CH = 256
VMEM = pl.BlockSpec(memory_space=pltpu.VMEM)


def nt(a, b):
    return lax.dot_general(a, b, (((1,), (1,)), ((), ())), preferred_element_type=jnp.float32)


def tn(a, b):
    return lax.dot_general(a, b, (((0,), (0,)), ((), ())), preferred_element_type=jnp.float32)


def nn(a, b):
    return jnp.dot(a, b, preferred_element_type=jnp.float32)


def place():
    r, e = lax.axis_index("dp"), lax.axis_index("expert")
    return r, e // NX, lax.rem(e, NX)


def enter(r, z, x):
    barrier = pltpu.get_barrier_semaphore()
    for dz in (1, NZ - 1):
        pl.semaphore_signal(barrier, inc=1, device_id=(r, lax.rem(z + dz, NZ) * NX + x), device_id_type=MESH)
    for dx in range(1, NX):
        pl.semaphore_signal(barrier, inc=1, device_id=(r, z * NX + lax.rem(x + dx, NX)), device_id_type=MESH)
    pl.semaphore_wait(barrier, NX + 1)


def build_picker(z, meta, pick, slot_gate):
    ids = meta[:, 0:8, :]
    gates = meta[:, 8:16, :]
    upper = (
        lax.broadcasted_iota(jnp.int32, (BLK, BLK), 0) < lax.broadcasted_iota(jnp.int32, (BLK, BLK), 1)
    ).astype(jnp.bfloat16)
    row = lax.broadcasted_iota(jnp.int32, (GRP, BLK), 0)
    base = lax.broadcasted_iota(jnp.int32, (NZ, BLK), 0) * CAP
    for xp in range(NX):
        same = ids == (z * NX + xp).astype(jnp.float32)
        named = jnp.sum(jnp.where(same, 1.0, 0.0), axis=1)
        gate = jnp.sum(jnp.where(same, gates, 0.0), axis=1)
        earlier = nn(named.astype(jnp.bfloat16), upper).astype(jnp.int32)
        key = jnp.where(named > 0.5, base + earlier, -1)
        total = jnp.zeros((GRP, BLK), jnp.float32)
        for zz in range(NZ):
            hit = row == key[zz : zz + 1, :]
            pick[xp * GRP : (xp + 1) * GRP, zz * BLK : (zz + 1) * BLK] = jnp.where(hit, 1.0, 0.0).astype(jnp.bfloat16)
            total = total + jnp.where(hit, gate[zz : zz + 1, :], 0.0)
        slot_gate[xp * GRP : (xp + 1) * GRP, :] = jnp.sum(total, axis=1, keepdims=True)


def dispatch_kernel(
    cot, tok, own_meta, slot, pick, ag, meta, stage, slot_gate, z_send, z_recv, m_send, m_recv, x_send, x_recv
):
    r, z, x = place()
    half_chunks = cot.shape[1] // CH
    chunks = 2 * half_chunks
    enter(r, z, x)
    sides = ((1, (r, lax.rem(z + 1, NZ) * NX + x)), (NZ - 1, (r, lax.rem(z + NZ - 1, NZ) * NX + x)))
    mine = pl.ds(pl.multiple_of(z * BLK, BLK), BLK)
    meta[z] = own_meta[...]
    for j in range(half_chunks):
        ag[j, mine, :] = cot[:, j * CH : (j + 1) * CH]
        ag[half_chunks + j, mine, :] = tok[:, j * CH : (j + 1) * CH]

    def ring(i, j, s, dist):
        back, to = sides[i]
        origin = lax.rem(z + dist * (NZ - back), NZ)
        if s == 3:
            rows = pl.ds(pl.multiple_of(origin * BLK + i * (BLK // 2), BLK // 2), BLK // 2)
        else:
            rows = pl.ds(pl.multiple_of(origin * BLK, BLK), BLK)
        view = ag.at[j, rows, :]
        return pltpu.make_async_remote_copy(
            src_ref=view, dst_ref=view, send_sem=z_send.at[i, j, s], recv_sem=z_recv.at[i, j, s],
            device_id=to, device_id_type=MESH,
        )

    def ring_meta(i, s, dist):
        back, to = sides[i]
        origin = lax.rem(z + dist * (NZ - back), NZ)
        view = meta.at[origin, i * 8 : i * 8 + 8, :] if s == 3 else meta.at[origin]
        return pltpu.make_async_remote_copy(
            src_ref=view, dst_ref=view, send_sem=m_send.at[i, s], recv_sem=m_recv.at[i, s],
            device_id=to, device_id_type=MESH,
        )

    def exchange(j, d):
        to = lax.rem(x + d, NX)
        return pltpu.make_async_remote_copy(
            src_ref=stage.at[j, pl.ds(pl.multiple_of(to * GRP, 16), GRP), :],
            dst_ref=slot.at[j, pl.ds(pl.multiple_of(x * GRP, 16), GRP), :],
            send_sem=x_send.at[j, d - 1], recv_sem=x_recv.at[j, d - 1],
            device_id=(r, z * NX + to), device_id_type=MESH,
        )

    def arrival(j, d):
        src = lax.rem(x + NX - d, NX)
        view = slot.at[j, pl.ds(pl.multiple_of(src * GRP, 16), GRP), :]
        return pltpu.make_async_remote_copy(
            src_ref=view, dst_ref=view, send_sem=x_send.at[j, d - 1], recv_sem=x_recv.at[j, d - 1],
            device_id=(r, z * NX + src), device_id_type=MESH,
        )

    def tick(t, carry):
        for s in (4, 3, 2, 1, 0):
            j = t - s

            @pl.when((j >= 0) & (j < chunks))
            def _():
                if s > 0:

                    @pl.when(j == 0)
                    def _():
                        for i in range(2):
                            ring_meta(i, s - 1, s).wait_recv()
                            if s < 4:
                                ring_meta(i, s, s).start()

                    for i in range(2):
                        ring(i, j, s - 1, s).wait_recv()
                        if s < 4:
                            ring(i, j, s, s).start()
                else:

                    @pl.when(j == 0)
                    def _():
                        for i in range(2):
                            ring_meta(i, 0, 0).start()

                    for i in range(2):
                        ring(i, j, 0, 0).start()

        j = t - 4

        @pl.when(j == 0)
        def _():
            build_picker(z, meta, pick, slot_gate)

        @pl.when(j >= 0)
        def _():
            plain = (j >= half_chunks).astype(jnp.float32)
            for d in (2, 1, 3, 0):
                to = lax.rem(x + d, NX)
                rows = pl.ds(pl.multiple_of(to * GRP, 16), GRP)
                gate = slot_gate[rows, :]
                value = nn(pick[rows, :], ag[j])
                value = (value * (gate * (1.0 - plain) + plain)).astype(jnp.bfloat16)
                if d == 0:
                    slot[j, rows, :] = value
                else:
                    stage[j, rows, :] = value
                    exchange(j, d).start()

        return carry

    lax.fori_loop(0, chunks + 4, tick, 0)
    for i in range(2):
        for s in range(4):
            ring_meta(i, s, s).wait_send()

    def finish(j, carry):
        for i in range(2):
            for s in range(4):
                ring(i, j, s, s).wait_send()
        for d in (2, 1, 3):
            exchange(j, d).wait_send()
            arrival(j, d).wait_recv()
        return carry

    lax.fori_loop(0, chunks, finish, 0)


def middle_kernel(slot, pre, w_gate, w_up, w_down, back, p_gate, p_up, p_down, gh, g_gate, g_up, hidden_t):
    hidden = w_gate.shape[2]
    chunks = w_gate.shape[0]
    for g in range(NX):
        rows = slice(g * GRP, (g + 1) * GRP)
        gh[rows, :] = jnp.zeros((GRP, hidden), jnp.float32)

    def down(j, carry):
        for g in range(NX):
            rows = slice(g * GRP, (g + 1) * GRP)
            gh[rows, :] += nt(slot[j, rows, :], w_down[j])
        return carry

    lax.fori_loop(0, chunks, down, 0)
    acts = []
    for g in range(NX):
        rows = slice(g * GRP, (g + 1) * GRP)
        gate = pre[rows, :hidden].astype(jnp.float32)
        up = pre[rows, hidden:].astype(jnp.float32)
        sig = 1.0 / (1.0 + jnp.exp(-gate))
        grad = gh[rows, :]
        g_gate[rows, :] = (grad * up * sig * (1.0 + gate * (1.0 - sig))).astype(jnp.bfloat16)
        g_up[rows, :] = (grad * gate * sig).astype(jnp.bfloat16)
        acts.append((gate * sig * up).astype(jnp.bfloat16))
    hidden_t[...] = jnp.concatenate(acts, axis=0).T

    def rest(j, carry):
        for g in range(NX):
            rows = slice(g * GRP, (g + 1) * GRP)
            back[j, rows, :] = (nt(g_gate[rows, :], w_gate[j]) + nt(g_up[rows, :], w_up[j])).astype(jnp.bfloat16)
        p_gate[j] = tn(slot[chunks + j], g_gate[...]).astype(jnp.bfloat16)
        p_up[j] = tn(slot[chunks + j], g_up[...]).astype(jnp.bfloat16)
        p_down[j] = nn(hidden_t[...], slot[j]).astype(jnp.bfloat16)
        return carry

    lax.fori_loop(0, chunks, rest, 0)


def combine_kernel(back, pick, out, landed, part, z_out, z_in, z_send, z_recv, x_send, x_recv):
    r, z, x = place()
    chunks = back.shape[0]
    enter(r, z, x)
    sides = ((1, (r, lax.rem(z + 1, NZ) * NX + x)), (NZ - 1, (r, lax.rem(z + NZ - 1, NZ) * NX + x)))

    def exchange(j, d):
        to = lax.rem(x + d, NX)
        return pltpu.make_async_remote_copy(
            src_ref=back.at[j, pl.ds(pl.multiple_of(to * GRP, 16), GRP), :],
            dst_ref=landed.at[j, pl.ds(pl.multiple_of(x * GRP, 16), GRP), :],
            send_sem=x_send.at[j, d - 1], recv_sem=x_recv.at[j, d - 1],
            device_id=(r, z * NX + to), device_id_type=MESH,
        )

    def arrival(j, d):
        src = lax.rem(x + NX - d, NX)
        view = landed.at[j, pl.ds(pl.multiple_of(src * GRP, 16), GRP), :]
        return pltpu.make_async_remote_copy(
            src_ref=view, dst_ref=view, send_sem=x_send.at[j, d - 1], recv_sem=x_recv.at[j, d - 1],
            device_id=(r, z * NX + src), device_id_type=MESH,
        )

    def ring(i, j, s):
        to = sides[i][1]
        rows = pl.ds(0, BLK // 2) if s == 0 else pl.ds(0, BLK)
        return pltpu.make_async_remote_copy(
            src_ref=z_out.at[i, j, s, rows, :], dst_ref=z_in.at[i, j, s, rows, :],
            send_sem=z_send.at[i, j, s], recv_sem=z_recv.at[i, j, s], device_id=to, device_id_type=MESH,
        )

    def start(j, carry):
        for d in (2, 1, 3):
            exchange(j, d).start()
        own = pl.ds(pl.multiple_of(x * GRP, 16), GRP)
        landed[j, own, :] = back[j, own, :]
        return carry

    lax.fori_loop(0, chunks, start, 0)

    def tick(t, carry):
        for s in (4, 3, 2, 1):
            j = t - s

            @pl.when((j >= 0) & (j < chunks))
            def _():
                if s == 4:
                    for i in range(2):
                        ring(i, j, 3).wait_recv()
                    mine = pl.ds(pl.multiple_of(z * BLK, BLK), BLK)
                    total = part[j, mine, :] + z_in[0, j, 3].astype(jnp.float32) + z_in[1, j, 3].astype(jnp.float32)
                    out[j] = total.astype(jnp.bfloat16)
                else:
                    for i in range(2):
                        step = sides[i][0]
                        dest = lax.rem(z + step * (4 - s), NZ)
                        ring(i, j, s - 1).wait_recv()
                        if s == 1:
                            h = BLK // 2
                            for k in range(2):
                                value = part[j, pl.ds(pl.multiple_of(dest * BLK + k * h, h), h), :]
                                if k == i:
                                    value = value + z_in[i, j, 0, 0:h, :].astype(jnp.float32)
                                z_out[i, j, 1, k * h : (k + 1) * h, :] = value.astype(jnp.bfloat16)
                        else:
                            value = part[j, pl.ds(pl.multiple_of(dest * BLK, BLK), BLK), :]
                            z_out[i, j, s] = (value + z_in[i, j, s - 1].astype(jnp.float32)).astype(jnp.bfloat16)
                        ring(i, j, s).start()

        @pl.when(t < chunks)
        def _():
            for d in (2, 1, 3):
                arrival(t, d).wait_recv()
            part[t] = tn(pick[...], landed[t])
            h = BLK // 2
            dest = lax.rem(z + 4, NZ)
            for i in range(2):
                z_out[i, t, 0, 0:h, :] = part[t, pl.ds(pl.multiple_of(dest * BLK + i * h, h), h), :].astype(jnp.bfloat16)
                ring(i, t, 0).start()

        return carry

    lax.fori_loop(0, chunks + 4, tick, 0)

    def finish(j, carry):
        for i in range(2):
            for s in range(4):
                ring(i, j, s).wait_send()
        for d in (2, 1, 3):
            exchange(j, d).wait_send()
        return carry

    lax.fori_loop(0, chunks, finish, 0)


def shards(tokens, cotangent, expert_ids, gate_values, saved_pre, w_gate, w_up, w_down):
    width = tokens.shape[1]
    hidden = w_gate.shape[2]
    chunks = width // CH
    dma = pltpu.SemaphoreType.DMA
    bf = jnp.bfloat16
    gate_full = lax.all_gather(w_gate[0], "dp", axis=0)
    up_full = lax.all_gather(w_up[0], "dp", axis=0)
    down_full = lax.all_gather(w_down[0], "dp", axis=0)
    meta = jnp.concatenate(
        [
            jnp.pad(expert_ids.astype(jnp.float32).T, ((0, 2), (0, 0)), constant_values=-1.0),
            jnp.pad(gate_values.T, ((0, 2), (0, 0))),
        ],
        axis=0,
    )
    pre = saved_pre.reshape(NZ, NX, CAP, 2 * hidden).transpose(1, 0, 2, 3).reshape(SLOTS, 2 * hidden)
    slot, pick = pl.pallas_call(
        dispatch_kernel,
        out_shape=(
            jax.ShapeDtypeStruct((2 * chunks, SLOTS, CH), bf),
            jax.ShapeDtypeStruct((SLOTS, NZ * BLK), bf),
        ),
        in_specs=[VMEM] * 3,
        out_specs=(VMEM, VMEM),
        scratch_shapes=[
            pltpu.VMEM((2 * chunks, NZ * BLK, CH), bf),
            pltpu.VMEM((NZ, 16, BLK), jnp.float32),
            pltpu.VMEM((2 * chunks, SLOTS, CH), bf),
            pltpu.VMEM((SLOTS, 1), jnp.float32),
            dma((2, 2 * chunks, 4)),
            dma((2, 2 * chunks, 4)),
            dma((2, 4)),
            dma((2, 4)),
            dma((2 * chunks, 3)),
            dma((2 * chunks, 3)),
        ],
        compiler_params=pltpu.CompilerParams(
            collective_id=0, has_side_effects=True, vmem_limit_bytes=40 * 2**20
        ),
        cost_estimate=pl.CostEstimate(flops=7 * 10**9, bytes_accessed=10 * 2**20, transcendentals=0),
        name="dispatch",
    )(cotangent, tokens, meta)
    back, p_gate, p_up, p_down = pl.pallas_call(
        middle_kernel,
        out_shape=(
            jax.ShapeDtypeStruct((chunks, SLOTS, CH), bf),
            jax.ShapeDtypeStruct((chunks, CH, hidden), bf),
            jax.ShapeDtypeStruct((chunks, CH, hidden), bf),
            jax.ShapeDtypeStruct((chunks, hidden, CH), bf),
        ),
        in_specs=[VMEM] * 5,
        out_specs=(VMEM,) * 4,
        scratch_shapes=[
            pltpu.VMEM((SLOTS, hidden), jnp.float32),
            pltpu.VMEM((SLOTS, hidden), bf),
            pltpu.VMEM((SLOTS, hidden), bf),
            pltpu.VMEM((hidden, SLOTS), bf),
        ],
        compiler_params=pltpu.CompilerParams(vmem_limit_bytes=56 * 2**20),
        cost_estimate=pl.CostEstimate(flops=15 * 10**9, bytes_accessed=30 * 2**20, transcendentals=10**6),
        name="middle",
    )(slot, pre, gate_full, up_full, down_full)
    out = pl.pallas_call(
        combine_kernel,
        out_shape=jax.ShapeDtypeStruct((chunks, BLK, CH), bf),
        in_specs=[VMEM] * 2,
        out_specs=VMEM,
        scratch_shapes=[
            pltpu.VMEM((chunks, SLOTS, CH), bf),
            pltpu.VMEM((chunks, NZ * BLK, CH), jnp.float32),
            pltpu.VMEM((2, chunks, 4, BLK, CH), bf),
            pltpu.VMEM((2, chunks, 4, BLK, CH), bf),
            dma((2, chunks, 4)),
            dma((2, chunks, 4)),
            dma((chunks, 3)),
            dma((chunks, 3)),
        ],
        compiler_params=pltpu.CompilerParams(
            collective_id=1, has_side_effects=True, vmem_limit_bytes=40 * 2**20
        ),
        cost_estimate=pl.CostEstimate(flops=4 * 10**9, bytes_accessed=6 * 2**20, transcendentals=0),
        name="combine",
    )(back, pick)
    grad_tokens = out.transpose(1, 0, 2).reshape(BLK, width)
    grads = [
        lax.psum_scatter(p, "dp", scatter_dimension=0, tiled=True) for p in (p_gate, p_up, p_down)
    ]
    return (grad_tokens, *grads)


def solution(mesh):
    tok = P(("dp", "expert"), None)
    row = P("expert", "dp", None)
    col = P("expert", None, "dp")
    return jax.shard_map(
        shards,
        mesh=mesh,
        in_specs=(tok, tok, tok, tok, P("expert", "dp", None, None, None), row, row, col),
        out_specs=(tok, row, row, col),
        check_vma=False,
    )
```

```python
import jax
import jax.numpy as jnp
from jax import lax
from jax.experimental import pallas as pl
from jax.experimental.pallas import tpu as pltpu
from jax.sharding import PartitionSpec as P

MESH = pl.DeviceIdType.MESH
NZ, NX, NY = 8, 4, 4
CAP = 26
BLK = 128
GRP = NZ * CAP
SLOTS = NX * GRP
CH = 256
VIA = 112
KEEP = 5
HALF = BLK // 2
BF = jnp.bfloat16
F32 = jnp.float32


def nt(a, b):
    return lax.dot_general(a, b, (((1,), (1,)), ((), ())), preferred_element_type=F32)


def tn(a, b):
    return lax.dot_general(a, b, (((0,), (0,)), ((), ())), preferred_element_type=F32)


def nn(a, b):
    return jnp.dot(a, b, preferred_element_type=F32)


def span(start, size, unit):
    return pl.ds(pl.multiple_of(start, unit), size)


def build_picker(z, meta, pick, slot_gate):
    ids = meta[:, 0:8, :]
    gates = meta[:, 8:16, :]
    upper = (
        lax.broadcasted_iota(jnp.int32, (BLK, BLK), 0) < lax.broadcasted_iota(jnp.int32, (BLK, BLK), 1)
    ).astype(BF)
    row = lax.broadcasted_iota(jnp.int32, (GRP, BLK), 0)
    base = lax.broadcasted_iota(jnp.int32, (NZ, BLK), 0) * CAP
    for xp in range(NX):
        same = ids == (z * NX + xp).astype(F32)
        named = jnp.sum(jnp.where(same, 1.0, 0.0), axis=1)
        gate = jnp.sum(jnp.where(same, gates, 0.0), axis=1)
        earlier = nn(named.astype(BF), upper).astype(jnp.int32)
        key = jnp.where(named > 0.5, base + earlier, -1)
        total = jnp.zeros((GRP, BLK), F32)
        for zz in range(NZ):
            hit = row == key[zz : zz + 1, :]
            pick[xp * GRP : (xp + 1) * GRP, zz * BLK : (zz + 1) * BLK] = jnp.where(hit, 1.0, 0.0).astype(BF)
            total = total + jnp.where(hit, gate[zz : zz + 1, :], 0.0)
        slot_gate[xp * GRP : (xp + 1) * GRP, :] = jnp.sum(total, axis=1, keepdims=True)


def kernel(
    cot, tok, own_meta, pre, w_gate, w_up, w_down, out, grad_gate, grad_up, grad_down,
    meta, ag, slot, stage, relay, pick, slot_gate, part, z_in, weights, gh, g_gate, g_up, hid, pre_in, pre32, tmp,
    sib_out, sib_in, y_out, y_half, y_full,
    z_send, z_recv, m_send, m_recv, x_send, x_recv, b_send, b_recv, w_send, w_recv, s_send, s_recv, y_send, y_recv, p_sem,
):
    r, e = lax.axis_index("dp"), lax.axis_index("expert")
    y, c = r // 2, lax.rem(r, 2)
    z, x = e // NX, lax.rem(e, NX)
    hidden = w_gate.shape[1]
    n = cot.shape[1] // CH

    def at(yy=y, cc=c, zz=z, xx=x):
        return (yy * 2 + cc, zz * NX + xx)

    z_to = (at(zz=lax.rem(z + 1, NZ)), at(zz=lax.rem(z + NZ - 1, NZ)))
    x_to = (at(xx=lax.rem(x + 1, NX)), at(xx=lax.rem(x + NX - 1, NX)))
    y_to = (at(yy=lax.rem(y + 1, NY)), at(yy=lax.rem(y + NY - 1, NY)))
    sibling = at(cc=1 - c)
    z_step = (1, NZ - 1)
    barrier = pltpu.get_barrier_semaphore()
    peers = (*z_to, *x_to, *y_to, sibling)
    for peer in peers:
        pl.semaphore_signal(barrier, inc=1, device_id=peer, device_id_type=MESH)
    pl.semaphore_wait(barrier, len(peers))

    def send(src, dst, s_sem, r_sem, to):
        return pltpu.make_async_remote_copy(
            src_ref=src, dst_ref=dst, send_sem=s_sem, recv_sem=r_sem, device_id=to, device_id_type=MESH
        )

    def block_of(k):
        q = k // 2
        off = 2 - q + 3 * (q // 2) - 2 * (q // 3)
        core = c + (1 - 2 * c) * (1 - lax.rem(k, 2))
        return lax.rem(y + off, NY) * 2 + core

    def w_copy(m, what):
        mine = y * 2 + c
        low = lax.rem(y + NY - 1, NY) * 2 + c
        high = lax.rem(y + 1, NY) * 2 + c
        far = lax.rem(y + 2, NY) * 2 + c
        h = CH // 2
        view, to = (
            (weights.at[m, mine], y_to[0]),
            (weights.at[m, mine], y_to[1]),
            (weights.at[m, low, 0:h, :], y_to[0]),
            (weights.at[m, high, h : 2 * h, :], y_to[1]),
            (weights.at[m, mine], sibling),
            (weights.at[m, low], sibling),
            (weights.at[m, high], sibling),
            (weights.at[m, far], sibling),
        )[what]
        return send(view, view, w_send.at[m, what], w_recv.at[m, what], to)

    def w_arrival(m, what):
        low = lax.rem(y + NY - 1, NY)
        high = lax.rem(y + 1, NY)
        far = lax.rem(y + 2, NY)
        h = CH // 2
        view, source = (
            (weights.at[m, low * 2 + c], y_to[1]),
            (weights.at[m, high * 2 + c], y_to[0]),
            (weights.at[m, far * 2 + c, 0:h, :], y_to[1]),
            (weights.at[m, far * 2 + c, h : 2 * h, :], y_to[0]),
            (weights.at[m, y * 2 + 1 - c], sibling),
            (weights.at[m, low * 2 + 1 - c], sibling),
            (weights.at[m, high * 2 + 1 - c], sibling),
            (weights.at[m, far * 2 + 1 - c], sibling),
        )[what]
        return send(view, view, w_send.at[m, what], w_recv.at[m, what], source)

    def w_start(m):
        for what in (0, 1, 4):
            w_copy(m, what).start()

    def w_forward(m):
        for i in range(2):
            w_arrival(m, i).wait_recv()
            w_copy(m, 2 + i).start()
            w_copy(m, 5 + i).start()

    def w_far(m):
        for i in range(2):
            w_arrival(m, 2 + i).wait_recv()
        w_copy(m, 7).start()

    def w_done(m):
        for what in range(4, 8):
            w_arrival(m, what).wait_recv()

    def ring(i, j, s, dist):
        origin = lax.rem(z + dist * (NZ - z_step[i]), NZ)
        rows = span(origin * BLK + i * HALF, HALF, HALF) if s == 3 else span(origin * BLK, BLK, BLK)
        view = ag.at[lax.rem(j, n), rows, :]
        return send(view, view, z_send.at[i, j, s], z_recv.at[i, j, s], z_to[i])

    def ring_meta(i, s, dist):
        origin = lax.rem(z + dist * (NZ - z_step[i]), NZ)
        view = meta.at[origin, i * 8 : i * 8 + 8, :] if s == 3 else meta.at[origin]
        return send(view, view, m_send.at[i, s], m_recv.at[i, s], z_to[i])

    def x_copy(j, what):
        i = what % 2
        st, sl, rl = lax.rem(j, 4), lax.rem(j, 2 * n), lax.rem(j, n)
        near = lax.rem(x + (1 if i == 0 else NX - 1), NX) * GRP
        far = lax.rem(x + 2, NX) * GRP
        other = lax.rem(x + (NX - 1 if i == 0 else 1), NX) * GRP
        lo, size = (0, VIA) if i == 0 else (VIA, GRP - VIA)
        if what < 2:
            src, dst = stage.at[st, span(near, GRP, 16), :], slot.at[sl, span(x * GRP, GRP, 16), :]
        elif what < 4:
            src, dst = stage.at[st, span(far + lo, size, 16), :], relay.at[rl, lo : lo + size, :]
        else:
            src, dst = relay.at[rl, lo : lo + size, :], slot.at[sl, span(other + lo, size, 16), :]
        return send(src, dst, x_send.at[j, what], x_recv.at[j, what], x_to[i])

    def x_arrival(j, what):
        i = what % 2
        sl, rl = lax.rem(j, 2 * n), lax.rem(j, n)
        other = lax.rem(x + (NX - 1 if i == 0 else 1), NX) * GRP
        far = lax.rem(x + 2, NX) * GRP
        lo, size = (0, VIA) if i == 0 else (VIA, GRP - VIA)
        if what < 2:
            view = slot.at[sl, span(other, GRP, 16), :]
        elif what < 4:
            view = relay.at[rl, lo : lo + size, :]
        else:
            view = slot.at[sl, span(far + lo, size, 16), :]
        return send(view, view, x_send.at[j, what], x_recv.at[j, what], x_to[1 - i])

    def back_out(i, k, s):
        return ag.at[k, (i * 4 + s) * BLK : (i * 4 + s) * BLK + (HALF if s == 0 else BLK), :]

    def back_ring(i, k, s):
        rows = slice(0, HALF if s == 0 else BLK)
        return send(back_out(i, k, s), z_in.at[i, k, s, rows, :], b_send.at[i, k, s], b_recv.at[i, k, s], z_to[i])

    def sib_copy(m, q):
        return send(sib_out.at[m], sib_in.at[m, q], s_send.at[m, q], s_recv.at[m, q], sibling)

    def y_copy(m, what):
        h = CH // 2
        src, dst, to = (
            (y_out.at[m, 0, 0:h, :], y_half.at[m, 0:h, :], y_to[0]),
            (y_out.at[m, 0, h : 2 * h, :], y_half.at[m, h : 2 * h, :], y_to[1]),
            (y_out.at[m, 1], y_full.at[m, 0], y_to[0]),
            (y_out.at[m, 0], y_full.at[m, 1], y_to[1]),
        )[what]
        return send(src, dst, y_send.at[m, what], y_recv.at[m, what], to)

    def reduce_block(m, k, chunk, act):
        q = k // 2
        h = CH // 2
        tmp[...] = tn(slot[chunk], act[...])

        @pl.when(lax.rem(k, 2) == 0)
        def _():
            @pl.when(q > 0)
            def _():
                sib_copy(m, q - 1).wait_send()

            sib_out[m] = tmp[...].astype(BF)
            sib_copy(m, q).start()

        @pl.when(lax.rem(k, 2) == 1)
        def _():
            sib_copy(m, q).wait_recv()
            tmp[...] += sib_in[m, q].astype(F32)

        @pl.when(k == 1)
        def _():
            y_out[m, 0] = tmp[...].astype(BF)
            y_copy(m, 0).start()
            y_copy(m, 1).start()

        @pl.when(k == 3)
        def _():
            y_copy(m, 0).wait_recv()
            tmp[0:h, :] += y_half[m, 0:h, :].astype(F32)
            y_out[m, 1] = tmp[...].astype(BF)
            y_copy(m, 2).start()

        @pl.when(k == 5)
        def _():
            y_copy(m, 0).wait_send()
            y_copy(m, 1).wait_send()
            y_copy(m, 1).wait_recv()
            tmp[h : 2 * h, :] += y_half[m, h : 2 * h, :].astype(F32)
            y_out[m, 0] = tmp[...].astype(BF)
            y_copy(m, 3).start()

        @pl.when(k == 7)
        def _():
            y_copy(m, 2).wait_recv()
            y_copy(m, 3).wait_recv()
            total = tmp[...] + y_full[m, 0].astype(F32) + y_full[m, 1].astype(F32)
            if m == 0:
                grad_down[...] = total.T.astype(BF)
            else:
                (grad_gate, grad_up)[m - 1][...] = total.astype(BF)

    def pre_copy(g):
        return pltpu.make_async_copy(pre.at[:, g], pre_in.at[g % 2], p_sem.at[g])

    def activations(g):
        pre_copy(g).wait()
        for zz in range(NZ):
            pre32[zz * CAP : (zz + 1) * CAP, :] = pre_in[g % 2, zz].astype(F32)
        if g + 2 < NX:
            pre_copy(g + 2).start()

        def rows16(b, carry):
            src = span(b * 16, 16, 16)
            dst = span(g * GRP + b * 16, 16, 16)
            gate, up = pre32[src, :hidden], pre32[src, hidden:]
            sig = 1.0 / (1.0 + jnp.exp(-gate))
            g_gate[dst, :] = (up * sig * (1.0 + gate * (1.0 - sig))).astype(BF)
            g_up[dst, :] = (gate * sig).astype(BF)
            hid[dst, :] = (gate * sig * up).astype(BF)
            return carry

        lax.fori_loop(0, GRP // 16, rows16, 0)
        gh[g * GRP : (g + 1) * GRP, :] = jnp.zeros((GRP, hidden), F32)

    pre_copy(0).start()
    pre_copy(1).start()
    mine = span(z * BLK, BLK, BLK)
    meta[z] = own_meta[...]
    own = y * 2 + c
    weights[0, own] = w_down[...].T
    w_start(0)
    weights[1, own] = w_gate[...]
    weights[2, own] = w_up[...]

    def tick(t, carry):
        for s in (4, 3, 2, 1, 0):
            j = t - s

            @pl.when((j >= 0) & (j < 2 * n))
            def _():
                if s > 0:

                    @pl.when(j == 0)
                    def _():
                        for i in range(2):
                            ring_meta(i, s - 1, s).wait_recv()
                            if s < 4:
                                ring_meta(i, s, s).start()

                    for i in range(2):
                        ring(i, j, s - 1, s).wait_recv()
                        if s < 4:
                            ring(i, j, s, s).start()
                else:

                    @pl.when(j == 0)
                    def _():
                        for i in range(2):
                            ring_meta(i, 0, 0).start()

                    columns = span(block_of(lax.rem(j, n)) * CH, CH, CH)

                    @pl.when(j < n)
                    def _():
                        ag[lax.rem(j, n), mine, :] = cot[:, columns]

                    @pl.when(j >= n)
                    def _():
                        ag[lax.rem(j, n), mine, :] = tok[:, columns]

                    for i in range(2):
                        ring(i, j, 0, 0).start()

        for s in (4, 3, 2, 1):
            k = t - (2 * n + 6) - s
            kp = lax.rem(k + KEEP, KEEP)

            @pl.when((k >= 0) & (k < n))
            def _():
                if s == 4:
                    for i in range(2):
                        back_ring(i, k, 3).wait_recv()
                    total = part[kp, mine, :] + z_in[0, k, 3].astype(F32) + z_in[1, k, 3].astype(F32)
                    out[:, span(block_of(k) * CH, CH, CH)] = total.astype(BF)
                else:
                    for i in range(2):
                        dest = lax.rem(z + z_step[i] * (4 - s), NZ)
                        back_ring(i, k, s - 1).wait_recv()
                        base = (i * 4 + s) * BLK
                        if s == 1:
                            for p in range(2):
                                value = part[kp, span(dest * BLK + p * HALF, HALF, HALF), :]
                                if p == i:
                                    value = value + z_in[i, k, 0, 0:HALF, :].astype(F32)
                                ag[k, base + p * HALF : base + (p + 1) * HALF, :] = value.astype(BF)
                        else:
                            value = part[kp, span(dest * BLK, BLK, BLK), :]
                            ag[k, base : base + BLK, :] = (value + z_in[i, k, s - 1].astype(F32)).astype(BF)
                        back_ring(i, k, s).start()

        jr = t - 5

        @pl.when((jr >= 0) & (jr < 3 * n))
        def _():
            for i in range(2):
                x_arrival(jr, 2 + i).wait_recv()
                x_copy(jr, 4 + i).start()

        @pl.when((jr >= 0) & (jr < 2 * n))
        def _():
            for i in range(2):
                for s in range(4):
                    ring(i, jr, s, s).wait_send()

        j = t - 4

        @pl.when(j == 0)
        def _():
            build_picker(z, meta, pick, slot_gate)

        @pl.when((j >= 4) & (j < 3 * n))
        def _():
            for what in range(4):
                x_copy(j - 4, what).wait_send()

        def put(d, rows, value):
            if d == 0:
                slot[lax.rem(j, 2 * n), rows, :] = value
            else:
                stage[lax.rem(j, 4), rows, :] = value
            for what in {2: (2, 3), 1: (0,), 3: (1,), 0: ()}[d]:
                x_copy(j, what).start()

        @pl.when((j >= 0) & (j < 2 * n))
        def _():
            plain = (j >= n).astype(F32)
            for d in (2, 1, 3, 0):
                rows = span(lax.rem(x + d, NX) * GRP, GRP, 16)
                value = nn(pick[rows, :], ag[lax.rem(j, n)])
                put(d, rows, (value * (slot_gate[rows, :] * (1.0 - plain) + plain)).astype(BF))

        @pl.when((j >= 2 * n) & (j < 3 * n))
        def _():
            block = block_of(j - 2 * n)
            for d in (2, 1, 3, 0):
                rows = span(lax.rem(x + d, NX) * GRP, GRP, 16)
                put(d, rows, (nt(g_gate[rows, :], weights[1, block]) + nt(g_up[rows, :], weights[2, block])).astype(BF))

        ja = t - 6

        @pl.when((ja >= 0) & (ja < 3 * n))
        def _():
            for what in (0, 1, 4, 5):
                x_arrival(ja, what).wait_recv()

        @pl.when((ja >= 1) & (ja < 3 * n + 1))
        def _():
            for what in (4, 5):
                x_copy(ja - 1, what).wait_send()

        for when, step in (
            (2, lambda: (w_forward(0), w_start(1))),
            (4, lambda: w_far(0)),
            (5, lambda: (w_done(0), w_forward(1), w_start(2))),
            (7, lambda: w_far(1)),
            (8, lambda: w_forward(2)),
            (9, lambda: w_done(1)),
            (10, lambda: w_far(2)),
            (12, lambda: w_done(2)),
        ):

            @pl.when(t == when)
            def _():
                step()

        for g in range(NX):

            @pl.when(t == g)
            def _():
                activations(g)

        @pl.when((ja >= 0) & (ja < n))
        def _():
            block = block_of(ja)
            for g in range(NX):
                rows = slice(g * GRP, (g + 1) * GRP)
                gh[rows, :] += nn(slot[ja, rows, :], weights[0, block])

        @pl.when(ja == n - 1)
        def _():
            for g in range(NX):
                rows = slice(g * GRP, (g + 1) * GRP)
                g_gate[rows, :] = (gh[rows, :] * g_gate[rows, :].astype(F32)).astype(BF)
                g_up[rows, :] = (gh[rows, :] * g_up[rows, :].astype(F32)).astype(BF)

        @pl.when((ja >= 1) & (ja < n + 1))
        def _():
            reduce_block(0, ja - 1, ja - 1, hid)

        @pl.when((ja >= n) & (ja < 2 * n))
        def _():
            reduce_block(1, ja - n, ja, g_gate)
            reduce_block(2, ja - n, ja, g_up)

        @pl.when((ja >= 2 * n) & (ja < 3 * n))
        def _():
            k = ja - 2 * n
            kp = lax.rem(k, KEEP)
            part[kp] = tn(pick[...], slot[k])
            dest = lax.rem(z + 4, NZ)
            for i in range(2):
                value = part[kp, span(dest * BLK + i * HALF, HALF, HALF), :]
                ag[k, i * 4 * BLK : i * 4 * BLK + HALF, :] = value.astype(BF)
                back_ring(i, k, 0).start()

        return carry

    lax.fori_loop(0, 3 * n + 10, tick, 0)
    for i in range(2):
        for s in range(4):
            ring_meta(i, s, s).wait_send()

    def ended(k, carry):
        for i in range(2):
            for s in range(4):
                back_ring(i, k, s).wait_send()
        return carry

    lax.fori_loop(0, n, ended, 0)
    for j in range(3 * n - 4, 3 * n):
        for what in range(4):
            x_copy(j, what).wait_send()
    for m in range(3):
        for what in range(8):
            w_copy(m, what).wait_send()
        sib_copy(m, 3).wait_send()
        y_copy(m, 2).wait_send()
        y_copy(m, 3).wait_send()


def shards(tokens, cotangent, expert_ids, gate_values, saved_pre, w_gate, w_up, w_down):
    width = tokens.shape[1]
    hidden = w_gate.shape[2]
    n = width // CH
    dma = pltpu.SemaphoreType.DMA
    vmem = pl.BlockSpec(memory_space=pltpu.VMEM)
    meta = jnp.concatenate(
        [
            jnp.pad(expert_ids.astype(F32).T, ((0, 2), (0, 0)), constant_values=-1.0),
            jnp.pad(gate_values.T, ((0, 2), (0, 0))),
        ],
        axis=0,
    )
    pre = saved_pre.reshape(NZ, NX, CAP, 2 * hidden)
    out, grad_gate, grad_up, grad_down = pl.pallas_call(
        kernel,
        out_shape=(
            jax.ShapeDtypeStruct((BLK, width), BF),
            jax.ShapeDtypeStruct((CH, hidden), BF),
            jax.ShapeDtypeStruct((CH, hidden), BF),
            jax.ShapeDtypeStruct((hidden, CH), BF),
        ),
        in_specs=[vmem] * 3 + [pl.BlockSpec(memory_space=pl.ANY)] + [vmem] * 3,
        out_specs=(vmem,) * 4,
        scratch_shapes=[
            pltpu.VMEM((NZ, 16, BLK), F32),
            pltpu.VMEM((n, NZ * BLK, CH), BF),
            pltpu.VMEM((2 * n, SLOTS, CH), BF),
            pltpu.VMEM((4, SLOTS, CH), BF),
            pltpu.VMEM((n, GRP, CH), BF),
            pltpu.VMEM((SLOTS, NZ * BLK), BF),
            pltpu.VMEM((SLOTS, 1), F32),
            pltpu.VMEM((KEEP, NZ * BLK, CH), F32),
            pltpu.VMEM((2, n, 4, BLK, CH), BF),
            pltpu.VMEM((3, n, CH, hidden), BF),
            pltpu.VMEM((SLOTS, hidden), F32),
            pltpu.VMEM((SLOTS, hidden), BF),
            pltpu.VMEM((SLOTS, hidden), BF),
            pltpu.VMEM((SLOTS, hidden), BF),
            pltpu.VMEM((2, NZ, CAP, 2 * hidden), BF),
            pltpu.VMEM((GRP, 2 * hidden), F32),
            pltpu.VMEM((CH, hidden), F32),
            pltpu.VMEM((3, CH, hidden), BF),
            pltpu.VMEM((3, NY, CH, hidden), BF),
            pltpu.VMEM((3, 2, CH, hidden), BF),
            pltpu.VMEM((3, CH, hidden), BF),
            pltpu.VMEM((3, 2, CH, hidden), BF),
            dma((2, 2 * n, 4)),
            dma((2, 2 * n, 4)),
            dma((2, 4)),
            dma((2, 4)),
            dma((3 * n, 6)),
            dma((3 * n, 6)),
            dma((2, n, 4)),
            dma((2, n, 4)),
            dma((3, 8)),
            dma((3, 8)),
            dma((3, NY)),
            dma((3, NY)),
            dma((3, 4)),
            dma((3, 4)),
            dma((NX,)),
        ],
        compiler_params=pltpu.CompilerParams(
            collective_id=0, has_side_effects=True, vmem_limit_bytes=62 * 2**20
        ),
        cost_estimate=pl.CostEstimate(flops=26 * 10**9, bytes_accessed=10 * 2**20, transcendentals=10**6),
        name="expert_backward",
    )(cotangent, tokens, meta, pre, w_gate[0], w_up[0], w_down[0])
    return (out, grad_gate[None], grad_up[None], grad_down[None])


def solution(mesh):
    tok = P(("dp", "expert"), None)
    row = P("expert", "dp", None)
    col = P("expert", None, "dp")
    return jax.shard_map(
        shards,
        mesh=mesh,
        in_specs=(tok, tok, tok, tok, P("expert", "dp", None, None, None), row, row, col),
        out_specs=(tok, row, row, col),
        check_vma=False,
    )
```

```python
import jax
import jax.numpy as jnp
from jax import lax
from jax.experimental import pallas as pl
from jax.experimental.pallas import tpu as pltpu
from jax.sharding import PartitionSpec as P

MESH = pl.DeviceIdType.MESH
NZ, NX, NY = 8, 4, 4
CAP = 26
TOP = 6
BLK = 128
GRP = NZ * CAP
SLOTS = NX * GRP
CH = 256
VIA = 112
KEEP = 5
HALF = BLK // 2
BF = jnp.bfloat16
F32 = jnp.float32


def nt(a, b):
    return lax.dot_general(a, b, (((1,), (1,)), ((), ())), preferred_element_type=F32)


def tn(a, b):
    return lax.dot_general(a, b, (((0,), (0,)), ((), ())), preferred_element_type=F32)


def nn(a, b):
    return jnp.dot(a, b, preferred_element_type=F32)


def span(start, size, unit):
    return pl.ds(pl.multiple_of(start, unit), size)


def build_picker(z, meta, pick, slot_gate):
    ids = meta[:, 0:8, :]
    gates = meta[:, 8:16, :]
    upper = (
        lax.broadcasted_iota(jnp.int32, (BLK, BLK), 0) < lax.broadcasted_iota(jnp.int32, (BLK, BLK), 1)
    ).astype(BF)
    row = lax.broadcasted_iota(jnp.int32, (GRP, BLK), 0)
    base = lax.broadcasted_iota(jnp.int32, (NZ, BLK), 0)
    for xp in range(NX):
        same = ids == (z * NX + xp).astype(F32)
        named = jnp.sum(jnp.where(same, 1.0, 0.0), axis=1)
        gate = jnp.sum(jnp.where(same, gates, 0.0), axis=1)
        earlier = nn(named.astype(BF), upper).astype(jnp.int32)
        key = jnp.where(named > 0.5, base + earlier * NZ, -1)
        total = jnp.zeros((GRP, BLK), F32)
        for zz in range(NZ):
            hit = row == key[zz : zz + 1, :]
            pick[xp * GRP : (xp + 1) * GRP, zz * BLK : (zz + 1) * BLK] = jnp.where(hit, 1.0, 0.0).astype(BF)
            total = total + jnp.where(hit, gate[zz : zz + 1, :], 0.0)
        slot_gate[xp * GRP : (xp + 1) * GRP, :] = jnp.sum(total, axis=1, keepdims=True)


def kernel(
    cot, tok, ids, gates, pre, w_gate, w_up, w_down, out, grads,
    meta, ag, slot, stage, relay, pick, pick_t, slot_gate, part, z_in, weights, g_gate, g_up, hid, act_t,
    pre_in, pre32, tmp, rows32, sib_out, sib_in, y_out, y_half, y_full,
    z_send, z_recv, m_send, m_recv, x_send, x_recv, b_send, b_recv, w_send, w_recv, s_send, s_recv, y_send, y_recv, p_sem,
):
    r, e = lax.axis_index("dp"), lax.axis_index("expert")
    y, c = r // 2, lax.rem(r, 2)
    z, x = e // NX, lax.rem(e, NX)
    hidden = w_gate.shape[0]
    half_hid = hidden // 2
    n = cot.shape[1] // CH

    def at(yy=y, cc=c, zz=z, xx=x):
        return (yy * 2 + cc, zz * NX + xx)

    z_to = (at(zz=lax.rem(z + 1, NZ)), at(zz=lax.rem(z + NZ - 1, NZ)))
    x_to = (at(xx=lax.rem(x + 1, NX)), at(xx=lax.rem(x + NX - 1, NX)))
    y_to = (at(yy=lax.rem(y + 1, NY)), at(yy=lax.rem(y + NY - 1, NY)))
    sibling = at(cc=1 - c)
    z_step = (1, NZ - 1)
    low = lax.rem(y + NY - 1, NY)
    high = lax.rem(y + 1, NY)
    far_y = lax.rem(y + 2, NY)
    own = y * 2 + c
    upper_half, lower_half = slice(0, half_hid), slice(half_hid, hidden)
    barrier = pltpu.get_barrier_semaphore()
    peers = (*z_to, *x_to, *y_to, sibling)
    for peer in peers:
        pl.semaphore_signal(barrier, inc=1, device_id=peer, device_id_type=MESH)
    pl.semaphore_wait(barrier, len(peers))

    def send(src, dst, s_sem, r_sem, to):
        return pltpu.make_async_remote_copy(
            src_ref=src, dst_ref=dst, send_sem=s_sem, recv_sem=r_sem, device_id=to, device_id_type=MESH
        )

    def block_of(k):
        q = k // 2
        off = 2 - q + 3 * (q // 2) - 2 * (q // 3)
        core = c + (1 - 2 * c) * (1 - lax.rem(k, 2))
        return lax.rem(y + off, NY) * 2 + core

    def w_copy(m, what):
        view, to = (
            (weights.at[m, own], y_to[0]),
            (weights.at[m, own], y_to[1]),
            (weights.at[m, low * 2 + c, upper_half, :], y_to[0]),
            (weights.at[m, high * 2 + c, lower_half, :], y_to[1]),
            (weights.at[m, own], sibling),
            (weights.at[m, low * 2 + c], sibling),
            (weights.at[m, high * 2 + c], sibling),
            (weights.at[m, far_y * 2 + c], sibling),
        )[what]
        return send(view, view, w_send.at[m, what], w_recv.at[m, what], to)

    def w_arrival(m, what):
        view, source = (
            (weights.at[m, low * 2 + c], y_to[1]),
            (weights.at[m, high * 2 + c], y_to[0]),
            (weights.at[m, far_y * 2 + c, upper_half, :], y_to[1]),
            (weights.at[m, far_y * 2 + c, lower_half, :], y_to[0]),
            (weights.at[m, y * 2 + 1 - c], sibling),
            (weights.at[m, low * 2 + 1 - c], sibling),
            (weights.at[m, high * 2 + 1 - c], sibling),
            (weights.at[m, far_y * 2 + 1 - c], sibling),
        )[what]
        return send(view, view, w_send.at[m, what], w_recv.at[m, what], source)

    def w_start(m):
        for what in (0, 1, 4):
            w_copy(m, what).start()

    def w_forward(m):
        for i in range(2):
            w_arrival(m, i).wait_recv()
            w_copy(m, 2 + i).start()
            w_copy(m, 5 + i).start()

    def w_far(m):
        for i in range(2):
            w_arrival(m, 2 + i).wait_recv()
        w_copy(m, 7).start()

    def w_done(m):
        for what in range(4, 8):
            w_arrival(m, what).wait_recv()

    def ring(i, j, s, p, dist):
        origin = lax.rem(z + dist * (NZ - z_step[i]), NZ)
        jn = lax.rem(j, n)
        view = ag.at[jn, span(origin * BLK + p * HALF, HALF, HALF), :]
        return send(view, view, z_send.at[i, jn, s, p], z_recv.at[i, jn, s, p], z_to[i])

    def ring_meta(i, s, dist):
        origin = lax.rem(z + dist * (NZ - z_step[i]), NZ)
        view = meta.at[origin, i * 8 : i * 8 + 8, :] if s == 3 else meta.at[origin]
        return send(view, view, m_send.at[i, s], m_recv.at[i, s], z_to[i])

    def x_copy(j, what):
        i = what % 2
        st, sl, rl = lax.rem(j, 4), lax.rem(j, 2 * n), lax.rem(j, n)
        near = lax.rem(x + (1 if i == 0 else NX - 1), NX) * GRP
        far = lax.rem(x + 2, NX) * GRP
        other = lax.rem(x + (NX - 1 if i == 0 else 1), NX) * GRP
        lo, size = (0, VIA) if i == 0 else (VIA, GRP - VIA)
        if what < 2:
            src, dst = stage.at[st, span(near, GRP, 16), :], slot.at[sl, span(x * GRP, GRP, 16), :]
        elif what < 4:
            src, dst = stage.at[st, span(far + lo, size, 16), :], relay.at[rl, lo : lo + size, :]
        else:
            src, dst = relay.at[rl, lo : lo + size, :], slot.at[sl, span(other + lo, size, 16), :]
        return send(src, dst, x_send.at[rl, what], x_recv.at[rl, what], x_to[i])

    def x_arrival(j, what):
        i = what % 2
        sl, rl = lax.rem(j, 2 * n), lax.rem(j, n)
        other = lax.rem(x + (NX - 1 if i == 0 else 1), NX) * GRP
        far = lax.rem(x + 2, NX) * GRP
        lo, size = (0, VIA) if i == 0 else (VIA, GRP - VIA)
        if what < 2:
            view = slot.at[sl, span(other, GRP, 16), :]
        elif what < 4:
            view = relay.at[rl, lo : lo + size, :]
        else:
            view = slot.at[sl, span(far + lo, size, 16), :]
        return send(view, view, x_send.at[rl, what], x_recv.at[rl, what], x_to[1 - i])

    def back_out(i, k, s, p):
        first = (i * 4 + s) * BLK + p * HALF
        return ag.at[k, first : first + HALF, :]

    def back_ring(i, k, s, p):
        dst = z_in.at[i, k, s, p * HALF : (p + 1) * HALF, :]
        return send(back_out(i, k, s, p), dst, b_send.at[i, k, s, p], b_recv.at[i, k, s, p], z_to[i])

    def sib_copy(m, q):
        return send(sib_out.at[m], sib_in.at[m, q], s_send.at[m, q], s_recv.at[m, q], sibling)

    def y_copy(m, what):
        src, dst, to = (
            (y_out.at[m, 0, upper_half, :], y_half.at[m, upper_half, :], y_to[0]),
            (y_out.at[m, 0, lower_half, :], y_half.at[m, lower_half, :], y_to[1]),
            (y_out.at[m, 1], y_full.at[m, 0], y_to[0]),
            (y_out.at[m, 0], y_full.at[m, 1], y_to[1]),
        )[what]
        return send(src, dst, y_send.at[m, what], y_recv.at[m, what], to)

    def reduce_block(m, k, chunk):
        q = k // 2
        tmp[...] = nn(act_t[m], slot[chunk])

        @pl.when(lax.rem(k, 2) == 0)
        def _():
            @pl.when(q > 0)
            def _():
                sib_copy(m, q - 1).wait_send()

            sib_out[m] = tmp[...].astype(BF)
            sib_copy(m, q).start()

        @pl.when(lax.rem(k, 2) == 1)
        def _():
            sib_copy(m, q).wait_recv()
            tmp[...] += sib_in[m, q].astype(F32)

        @pl.when(k == 1)
        def _():
            y_out[m, 0] = tmp[...].astype(BF)
            y_copy(m, 0).start()
            y_copy(m, 1).start()

        @pl.when(k == 3)
        def _():
            y_copy(m, 0).wait_recv()
            tmp[upper_half, :] += y_half[m, upper_half, :].astype(F32)
            y_out[m, 1] = tmp[...].astype(BF)
            y_copy(m, 2).start()

        @pl.when(k == 5)
        def _():
            y_copy(m, 0).wait_send()
            y_copy(m, 1).wait_send()
            y_copy(m, 1).wait_recv()
            tmp[lower_half, :] += y_half[m, lower_half, :].astype(F32)
            y_out[m, 0] = tmp[...].astype(BF)
            y_copy(m, 3).start()

        @pl.when(k == 7)
        def _():
            y_copy(m, 2).wait_recv()
            y_copy(m, 3).wait_recv()
            grads[m] = (tmp[...] + y_full[m, 0].astype(F32) + y_full[m, 1].astype(F32)).astype(BF)

    depth = 16 * NX
    steps = SLOTS // depth

    def pre_copy(b):
        buf = lax.rem(b, 4)
        return pltpu.make_async_copy(pre.at[span(b * depth, depth, depth), :], pre_in.at[buf], p_sem.at[buf])

    def activations(b):
        pre_copy(b).wait()
        row = lax.broadcasted_iota(jnp.int32, (depth, depth), 0)
        column = lax.broadcasted_iota(jnp.int32, (depth, depth), 1)
        order = jnp.where(column == lax.rem(row, 16) * NX + row // 16, 1.0, 0.0).astype(BF)
        pre32[...] = nn(order, pre_in[lax.rem(b, 4)])

        @pl.when(b + 4 < steps)
        def _():
            pre_copy(b + 4).start()

        for xx in range(NX):
            src = slice(xx * 16, (xx + 1) * 16)
            gate, up = pre32[src, :hidden], pre32[src, hidden:]
            sig = 1.0 / (1.0 + jnp.exp(-gate))
            dst = span(xx * GRP + b * 16, 16, 16)
            g_gate[dst, :] = (up * sig * (1.0 + gate * (1.0 - sig))).astype(BF)
            g_up[dst, :] = (gate * sig).astype(BF)
            hid[dst, :] = (gate * sig * up).astype(BF)

    for b in range(4):
        pre_copy(b).start()
    mine = span(z * BLK, BLK, BLK)
    meta[z] = jnp.full(meta.shape[1:], -1.0, F32)
    meta[z, 0:TOP, :] = ids[...].astype(F32)
    meta[z, 8 : 8 + TOP, :] = gates[...]
    weights[0, own] = w_down[...]
    w_start(0)
    weights[1, own] = w_gate[...]
    weights[2, own] = w_up[...]
    tiles = [slice(b, min(b + CH, hidden)) for b in range(0, hidden, CH)]
    for b in range(len(tiles)):
        part[b, 0:SLOTS, :] = jnp.zeros((SLOTS, CH), F32)

    def sub_tick(t, p):
        for s in (4, 3, 2, 1, 0):
            j = t - s

            @pl.when((j >= 0) & (j < 2 * n))
            def _():
                if s > 0:
                    if p == 0:

                        @pl.when(j == 0)
                        def _():
                            for i in range(2):
                                ring_meta(i, s - 1, s).wait_recv()
                                if s < 4:
                                    ring_meta(i, s, s).start()

                    for i in range(2):
                        last = 3 if p == i else 2
                        if s - 1 <= last:
                            ring(i, j, s - 1, p, s).wait_recv()
                        if s <= last:
                            ring(i, j, s, p, s).start()
                else:
                    if p == 0:

                        @pl.when(j == 0)
                        def _():
                            for i in range(2):
                                ring_meta(i, 0, 0).start()

                        columns = span(block_of(lax.rem(j, n)) * CH, CH, CH)

                        @pl.when(j < n)
                        def _():
                            ag[lax.rem(j, n), mine, :] = cot[:, columns]

                        @pl.when(j >= n)
                        def _():
                            ag[lax.rem(j, n), mine, :] = tok[:, columns]

                    for i in range(2):
                        ring(i, j, 0, p, 0).start()

        for s in (4, 3, 2, 1):
            k = t - (2 * n + 6) - s
            kp = lax.rem(k + KEEP, KEEP)
            half = slice(p * HALF, (p + 1) * HALF)

            @pl.when((k >= 0) & (k < n))
            def _():
                if s == 4:
                    total = part[kp, span(z * BLK + p * HALF, HALF, HALF), :]
                    for i in range(2):
                        back_ring(i, k, 3, p).wait_recv()
                        total = total + z_in[i, k, 3, half, :].astype(F32)
                    out[half, span(block_of(k) * CH, CH, CH)] = total.astype(BF)
                else:
                    for i in range(2):
                        dest = lax.rem(z + z_step[i] * (4 - s), NZ)
                        value = part[kp, span(dest * BLK + p * HALF, HALF, HALF), :]
                        if s > 1 or p == i:
                            back_ring(i, k, s - 1, p).wait_recv()
                            value = value + z_in[i, k, s - 1, half, :].astype(F32)
                        back_out(i, k, s, p)[...] = value.astype(BF)
                        back_ring(i, k, s, p).start()

    def tick(t, carry):
        sub_tick(t, 0)

        ja = t - 6

        @pl.when((ja >= 0) & (ja < 3 * n))
        def _():
            for what in (0, 1, 4, 5):
                x_arrival(ja, what).wait_recv()

        @pl.when((ja >= 1) & (ja < 3 * n + 1))
        def _():
            for what in (4, 5):
                x_copy(ja - 1, what).wait_send()

        for when, step in (
            (3, lambda: (w_forward(0), w_start(1))),
            (5, lambda: w_far(0)),
            (6, lambda: (w_done(0), w_forward(1), w_start(2))),
            (8, lambda: w_far(1)),
            (9, lambda: w_forward(2)),
            (10, lambda: w_done(1)),
            (11, lambda: w_far(2)),
            (13, lambda: w_done(2)),
        ):

            @pl.when(t == when)
            def _():
                step()

        @pl.when(t < 4)
        def _():
            def some(q, carry):
                @pl.when(t * 4 + q < steps)
                def _():
                    activations(t * 4 + q)

                return carry

            lax.fori_loop(0, 4, some, 0)

        @pl.when(t == 4)
        def _():
            act_t[0] = hid[...].T

        @pl.when((t >= 5) & (t < 5 + NZ))
        def _():
            block = span((t - 5) * BLK, BLK, BLK)
            pick_t[block, :] = pick[:, block].T

        @pl.when((ja >= 0) & (ja < n))
        def _():
            block = block_of(ja)
            for b, cols in enumerate(tiles):
                part[b, 0:SLOTS, 0 : cols.stop - cols.start] += nt(slot[ja], weights[0, block, cols, :])

        @pl.when(ja == n - 1)
        def _():
            for b, cols in enumerate(tiles):
                grad = part[b, 0:SLOTS, 0 : cols.stop - cols.start]
                g_gate[:, cols] = (grad * g_gate[:, cols].astype(F32)).astype(BF)
                g_up[:, cols] = (grad * g_up[:, cols].astype(F32)).astype(BF)
            act_t[1] = g_gate[...].T
            act_t[2] = g_up[...].T

        @pl.when((ja >= 3) & (ja < n + 3))
        def _():
            reduce_block(0, ja - 3, ja - 3)

        @pl.when((ja >= n) & (ja < 2 * n))
        def _():
            reduce_block(1, ja - n, ja)
            reduce_block(2, ja - n, ja)

        @pl.when((ja >= 2 * n) & (ja < 3 * n))
        def _():
            k = ja - 2 * n
            kp = lax.rem(k, KEEP)
            part[kp] = nn(pick_t[...], slot[k])
            dest = lax.rem(z + 4, NZ)
            for i in range(2):
                value = part[kp, span(dest * BLK + i * HALF, HALF, HALF), :]
                back_out(i, k, 0, i)[...] = value.astype(BF)
                back_ring(i, k, 0, i).start()

        jr = t - 5

        @pl.when((jr >= 0) & (jr < 3 * n))
        def _():
            for i in range(2):
                x_arrival(jr, 2 + i).wait_recv()
                x_copy(jr, 4 + i).start()

        @pl.when((jr >= 0) & (jr < 2 * n))
        def _():
            for i in range(2):
                for p in range(2):
                    for s in range(4 if p == i else 3):
                        ring(i, jr, s, p, s).wait_send()

        sub_tick(t, 1)

        j = t - 4

        @pl.when(j == 0)
        def _():
            build_picker(z, meta, pick, slot_gate)

        @pl.when((j >= 4) & (j < 3 * n))
        def _():
            for what in range(4):
                x_copy(j - 4, what).wait_send()

        @pl.when((j >= 0) & (j < 2 * n))
        def _():
            plain = (j >= n).astype(F32)
            rows32[...] = nn(pick[...], ag[lax.rem(j, n)]) * (slot_gate[...] * (1.0 - plain) + plain)

        @pl.when((j >= 2 * n) & (j < 3 * n))
        def _():
            block = block_of(j - 2 * n)
            rows32[...] = nn(g_gate[...], weights[1, block]) + nn(g_up[...], weights[2, block])

        @pl.when((j >= 0) & (j < 3 * n))
        def _():
            for d in (2, 1, 3, 0):
                rows = span(lax.rem(x + d, NX) * GRP, GRP, 16)
                if d == 0:
                    slot[lax.rem(j, 2 * n), rows, :] = rows32[rows, :].astype(BF)
                else:
                    stage[lax.rem(j, 4), rows, :] = rows32[rows, :].astype(BF)
                for what in {2: (2, 3), 1: (0,), 3: (1,), 0: ()}[d]:
                    x_copy(j, what).start()

        return carry

    lax.fori_loop(0, 3 * n + 10, tick, 0)
    for i in range(2):
        for s in range(4):
            ring_meta(i, s, s).wait_send()

    def ended(k, carry):
        for i in range(2):
            for p in range(2):
                for s in range(0 if p == i else 1, 4):
                    back_ring(i, k, s, p).wait_send()
        return carry

    lax.fori_loop(0, n, ended, 0)
    for j in range(3 * n - 4, 3 * n):
        for what in range(4):
            x_copy(j, what).wait_send()
    for m in range(3):
        for what in range(8):
            w_copy(m, what).wait_send()
        sib_copy(m, 3).wait_send()
        y_copy(m, 2).wait_send()
        y_copy(m, 3).wait_send()


def hand_out(rows, grads, out, grad_gate, grad_up, grad_down, sem):
    copies = [pltpu.make_async_copy(rows, out, sem.at[0])]
    for m, to in ((1, grad_gate), (2, grad_up), (0, grad_down)):
        copies.append(pltpu.make_async_copy(grads.at[m], to, sem.at[1 + m]))
    for copy in copies:
        copy.start()
    for copy in copies:
        copy.wait()


def shards(tokens, cotangent, expert_ids, gate_values, saved_pre, w_gate, w_up, w_down):
    width = tokens.shape[1]
    hidden = w_gate.shape[2]
    n = width // CH
    dma = pltpu.SemaphoreType.DMA
    vmem = pl.BlockSpec(memory_space=pltpu.VMEM)
    hbm = pl.BlockSpec(memory_space=pl.ANY)
    pre = saved_pre.reshape(NZ * NX, CAP, 2 * hidden).transpose(1, 0, 2).reshape(SLOTS, 2 * hidden)
    shape = jax.ShapeDtypeStruct
    rows, grads = pl.pallas_call(
        kernel,
        out_shape=(shape((BLK, width), BF), shape((3, hidden, CH), BF)),
        in_specs=[vmem] * 4 + [hbm] + [vmem] * 3,
        out_specs=(vmem, vmem),
        scratch_shapes=[
            pltpu.VMEM((NZ, 16, BLK), F32),
            pltpu.VMEM((n, NZ * BLK, CH), BF),
            pltpu.VMEM((2 * n, SLOTS, CH), BF),
            pltpu.VMEM((4, SLOTS, CH), BF),
            pltpu.VMEM((n, GRP, CH), BF),
            pltpu.VMEM((SLOTS, NZ * BLK), BF),
            pltpu.VMEM((NZ * BLK, SLOTS), BF),
            pltpu.VMEM((SLOTS, 1), F32),
            pltpu.VMEM((KEEP, NZ * BLK, CH), F32),
            pltpu.VMEM((2, n, 4, BLK, CH), BF),
            pltpu.VMEM((3, n, hidden, CH), BF),
            pltpu.VMEM((SLOTS, hidden), BF),
            pltpu.VMEM((SLOTS, hidden), BF),
            pltpu.VMEM((SLOTS, hidden), BF),
            pltpu.VMEM((3, hidden, SLOTS), BF),
            pltpu.VMEM((4, 16 * NX, 2 * hidden), BF),
            pltpu.VMEM((16 * NX, 2 * hidden), F32),
            pltpu.VMEM((hidden, CH), F32),
            pltpu.VMEM((SLOTS, CH), F32),
            pltpu.VMEM((3, hidden, CH), BF),
            pltpu.VMEM((3, NY, hidden, CH), BF),
            pltpu.VMEM((3, 2, hidden, CH), BF),
            pltpu.VMEM((3, hidden, CH), BF),
            pltpu.VMEM((3, 2, hidden, CH), BF),
            dma((2, n, 4, 2)),
            dma((2, n, 4, 2)),
            dma((2, 4)),
            dma((2, 4)),
            dma((n, 6)),
            dma((n, 6)),
            dma((2, n, 4, 2)),
            dma((2, n, 4, 2)),
            dma((3, 8)),
            dma((3, 8)),
            dma((3, NY)),
            dma((3, NY)),
            dma((3, 4)),
            dma((3, 4)),
            dma((4,)),
        ],
        compiler_params=pltpu.CompilerParams(
            collective_id=0, has_side_effects=True, vmem_limit_bytes=62 * 2**20
        ),
        cost_estimate=pl.CostEstimate(flops=26 * 10**9, bytes_accessed=10 * 2**20, transcendentals=10**6),
        name="expert_backward",
    )(cotangent, tokens, expert_ids.T, gate_values.T, pre, w_gate[0].T, w_up[0].T, w_down[0])
    out, grad_gate, grad_up, grad_down = pl.pallas_call(
        hand_out,
        out_shape=(shape((BLK, width), BF), *[shape((hidden, CH), BF)] * 3),
        in_specs=[hbm] * 2,
        out_specs=(hbm,) * 4,
        scratch_shapes=[dma((4,))],
        name="hand_out",
    )(rows, grads)
    return (out, grad_gate.T[None], grad_up.T[None], grad_down[None])


def solution(mesh):
    tok = P(("dp", "expert"), None)
    row = P("expert", "dp", None)
    col = P("expert", None, "dp")
    return jax.shard_map(
        shards,
        mesh=mesh,
        in_specs=(tok, tok, tok, tok, P("expert", "dp", None, None, None), row, row, col),
        out_specs=(tok, row, row, col),
        check_vma=False,
    )
```

```python
import jax
import jax.numpy as jnp
from jax import lax
from jax.experimental import pallas as pl
from jax.experimental.pallas import tpu as pltpu
from jax.sharding import PartitionSpec as P

MESH = pl.DeviceIdType.MESH
NZ, NX, NY = 8, 4, 4
CAP = 26
TOP = 6
BLK = 128
GRP = NZ * CAP
SLOTS = NX * GRP
CH = 256
VIA = 112
LAG = 2
X_LAG = 2
SUM_LAG = 2
AG_SLOTS = 12
HALF = BLK // 2
BF = jnp.bfloat16
F32 = jnp.float32


def nt(a, b):
    return lax.dot_general(a, b, (((1,), (1,)), ((), ())), preferred_element_type=F32)


def tn(a, b):
    return lax.dot_general(a, b, (((0,), (0,)), ((), ())), preferred_element_type=F32)


def nn(a, b):
    return jnp.dot(a, b, preferred_element_type=F32)


def span(start, size, unit):
    return pl.ds(pl.multiple_of(start, unit), size)


def build_picker(z, meta, pick, slot_gate):
    ids = meta[:, 0:8, :]
    gates = meta[:, 8:16, :]
    upper = (
        lax.broadcasted_iota(jnp.int32, (BLK, BLK), 0) < lax.broadcasted_iota(jnp.int32, (BLK, BLK), 1)
    ).astype(BF)
    row = lax.broadcasted_iota(jnp.int32, (GRP, BLK), 0)
    base = lax.broadcasted_iota(jnp.int32, (NZ, BLK), 0)
    for xp in range(NX):
        same = ids == (z * NX + xp).astype(F32)
        named = jnp.sum(jnp.where(same, 1.0, 0.0), axis=1)
        gate = jnp.sum(jnp.where(same, gates, 0.0), axis=1)
        earlier = nn(named.astype(BF), upper).astype(jnp.int32)
        key = jnp.where(named > 0.5, base + earlier * NZ, -1)
        total = jnp.zeros((GRP, BLK), F32)
        for zz in range(NZ):
            hit = row == key[zz : zz + 1, :]
            pick[xp * GRP : (xp + 1) * GRP, zz * BLK : (zz + 1) * BLK] = jnp.where(hit, 1.0, 0.0).astype(BF)
            total = total + jnp.where(hit, gate[zz : zz + 1, :], 0.0)
        slot_gate[xp * GRP : (xp + 1) * GRP, :] = jnp.sum(total, axis=1, keepdims=True)


def kernel(
    cot, tok, ids, gates, pre, w_gate, w_up, w_down, out, grads,
    meta, ag, slot, stage, relay, pick, pick_t, slot_gate, part, z_in, weights, gh, g_gate, g_up, act_t,
    pre_in, pre32, tmp, rows32, sib_out, sib_in, y_out, y_half, y_full,
    z_send, z_recv, m_send, m_recv, x_send, x_recv, b_send, b_recv, w_send, w_recv, s_send, s_recv, y_send, y_recv, p_sem,
):
    r, e = lax.axis_index("dp"), lax.axis_index("expert")
    y, c = r // 2, lax.rem(r, 2)
    z, x = e // NX, lax.rem(e, NX)
    hidden = w_gate.shape[0]
    half_hid = hidden // 2
    n = cot.shape[1] // CH

    def at(yy=y, cc=c, zz=z, xx=x):
        return (yy * 2 + cc, zz * NX + xx)

    z_to = (at(zz=lax.rem(z + 1, NZ)), at(zz=lax.rem(z + NZ - 1, NZ)))
    x_to = (at(xx=lax.rem(x + 1, NX)), at(xx=lax.rem(x + NX - 1, NX)))
    y_to = (at(yy=lax.rem(y + 1, NY)), at(yy=lax.rem(y + NY - 1, NY)))
    sibling = at(cc=1 - c)
    z_step = (1, NZ - 1)
    low = lax.rem(y + NY - 1, NY)
    high = lax.rem(y + 1, NY)
    far_y = lax.rem(y + 2, NY)
    own = y * 2 + c
    upper_half, lower_half = slice(0, half_hid), slice(half_hid, hidden)
    barrier = pltpu.get_barrier_semaphore()
    peers = (*z_to, *x_to, *y_to, sibling)
    for peer in peers:
        pl.semaphore_signal(barrier, inc=1, device_id=peer, device_id_type=MESH)
    pl.semaphore_wait(barrier, len(peers))

    def send(src, dst, s_sem, r_sem, to):
        return pltpu.make_async_remote_copy(
            src_ref=src, dst_ref=dst, send_sem=s_sem, recv_sem=r_sem, device_id=to, device_id_type=MESH
        )

    def block_of(k):
        q = k // 2
        off = 2 - q + 3 * (q // 2) - 2 * (q // 3)
        core = c + (1 - 2 * c) * (1 - lax.rem(k, 2))
        return lax.rem(y + off, NY) * 2 + core

    def w_copy(m, what):
        view, to = (
            (weights.at[m, own], y_to[0]),
            (weights.at[m, own], y_to[1]),
            (weights.at[m, low * 2 + c, upper_half, :], y_to[0]),
            (weights.at[m, high * 2 + c, lower_half, :], y_to[1]),
            (weights.at[m, own], sibling),
            (weights.at[m, low * 2 + c], sibling),
            (weights.at[m, high * 2 + c], sibling),
            (weights.at[m, far_y * 2 + c], sibling),
        )[what]
        return send(view, view, w_send.at[m, what], w_recv.at[m, what], to)

    def w_arrival(m, what):
        view, source = (
            (weights.at[m, low * 2 + c], y_to[1]),
            (weights.at[m, high * 2 + c], y_to[0]),
            (weights.at[m, far_y * 2 + c, upper_half, :], y_to[1]),
            (weights.at[m, far_y * 2 + c, lower_half, :], y_to[0]),
            (weights.at[m, y * 2 + 1 - c], sibling),
            (weights.at[m, low * 2 + 1 - c], sibling),
            (weights.at[m, high * 2 + 1 - c], sibling),
            (weights.at[m, far_y * 2 + 1 - c], sibling),
        )[what]
        return send(view, view, w_send.at[m, what], w_recv.at[m, what], source)

    def w_start(m):
        for what in (0, 1, 4):
            w_copy(m, what).start()

    def w_forward(m):
        for i in range(2):
            w_arrival(m, i).wait_recv()
            w_copy(m, 2 + i).start()
            w_copy(m, 5 + i).start()

    def w_far(m):
        for i in range(2):
            w_arrival(m, 2 + i).wait_recv()
        w_copy(m, 7).start()

    def w_done(m):
        for what in range(4, 8):
            w_arrival(m, what).wait_recv()

    def ring(i, j, s, dist):
        origin = lax.rem(z + dist * (NZ - z_step[i]), NZ)
        rows = span(origin * BLK + i * HALF, HALF, HALF) if s == 3 else span(origin * BLK, BLK, BLK)
        view = ag.at[lax.rem(j, AG_SLOTS), rows, :]
        return send(view, view, z_send.at[i, j, s], z_recv.at[i, j, s], z_to[i])

    def ring_meta(i, s, dist):
        origin = lax.rem(z + dist * (NZ - z_step[i]), NZ)
        view = meta.at[origin, i * 8 : i * 8 + 8, :] if s == 3 else meta.at[origin]
        return send(view, view, m_send.at[i, s], m_recv.at[i, s], z_to[i])

    def x_copy(j, what):
        i = what % 2
        st, sl, rl = lax.rem(j, 4), lax.rem(j, 2 * n), lax.rem(j, n)
        near = lax.rem(x + (1 if i == 0 else NX - 1), NX) * GRP
        far = lax.rem(x + 2, NX) * GRP
        other = lax.rem(x + (NX - 1 if i == 0 else 1), NX) * GRP
        lo, size = (0, VIA) if i == 0 else (VIA, GRP - VIA)
        if what < 2:
            src, dst = stage.at[st, span(near, GRP, 16), :], slot.at[sl, span(x * GRP, GRP, 16), :]
        elif what < 4:
            src, dst = stage.at[st, span(far + lo, size, 16), :], relay.at[rl, lo : lo + size, :]
        else:
            src, dst = relay.at[rl, lo : lo + size, :], slot.at[sl, span(other + lo, size, 16), :]
        return send(src, dst, x_send.at[rl, what], x_recv.at[rl, what], x_to[i])

    def x_arrival(j, what):
        i = what % 2
        sl, rl = lax.rem(j, 2 * n), lax.rem(j, n)
        other = lax.rem(x + (NX - 1 if i == 0 else 1), NX) * GRP
        far = lax.rem(x + 2, NX) * GRP
        lo, size = (0, VIA) if i == 0 else (VIA, GRP - VIA)
        if what < 2:
            view = slot.at[sl, span(other, GRP, 16), :]
        elif what < 4:
            view = relay.at[rl, lo : lo + size, :]
        else:
            view = slot.at[sl, span(far + lo, size, 16), :]
        return send(view, view, x_send.at[rl, what], x_recv.at[rl, what], x_to[1 - i])

    def back_out(i, k, s):
        first = (i * 4 + s) * BLK
        return ag.at[AG_SLOTS - n + k, first : first + (HALF if s == 0 else BLK), :]

    def back_ring(i, k, s):
        dst = z_in.at[i, k, s, 0 : HALF if s == 0 else BLK, :]
        return send(back_out(i, k, s), dst, b_send.at[i, k, s], b_recv.at[i, k, s], z_to[i])

    def sib_copy(m, q):
        return send(sib_out.at[m], sib_in.at[m, q], s_send.at[m, q], s_recv.at[m, q], sibling)

    def y_copy(m, what):
        src, dst, to = (
            (y_out.at[m, 0, upper_half, :], y_half.at[m, upper_half, :], y_to[0]),
            (y_out.at[m, 0, lower_half, :], y_half.at[m, lower_half, :], y_to[1]),
            (y_out.at[m, 1], y_full.at[m, 0], y_to[0]),
            (y_out.at[m, 0], y_full.at[m, 1], y_to[1]),
        )[what]
        return send(src, dst, y_send.at[m, what], y_recv.at[m, what], to)

    def reduce_block(m, k, chunk):
        q = k // 2
        tmp[...] = nn(act_t[m], slot[chunk])

        @pl.when(lax.rem(k, 2) == 0)
        def _():
            @pl.when(q > 0)
            def _():
                sib_copy(m, q - 1).wait_send()

            sib_out[m] = tmp[...].astype(BF)
            sib_copy(m, q).start()

        @pl.when(lax.rem(k, 2) == 1)
        def _():
            sib_copy(m, q).wait_recv()
            tmp[...] += sib_in[m, q].astype(F32)

        @pl.when(k == 1)
        def _():
            y_out[m, 0] = tmp[...].astype(BF)
            y_copy(m, 0).start()
            y_copy(m, 1).start()

        @pl.when(k == 3)
        def _():
            y_copy(m, 0).wait_recv()
            tmp[upper_half, :] += y_half[m, upper_half, :].astype(F32)
            y_out[m, 1] = tmp[...].astype(BF)
            y_copy(m, 2).start()

        @pl.when(k == 5)
        def _():
            y_copy(m, 0).wait_send()
            y_copy(m, 1).wait_send()
            y_copy(m, 1).wait_recv()
            tmp[lower_half, :] += y_half[m, lower_half, :].astype(F32)
            y_out[m, 0] = tmp[...].astype(BF)
            y_copy(m, 3).start()

        @pl.when(k == 7)
        def _():
            y_copy(m, 2).wait_recv()
            y_copy(m, 3).wait_recv()
            grads[m] = (tmp[...] + y_full[m, 0].astype(F32) + y_full[m, 1].astype(F32)).astype(BF)

    tiles = [slice(b, min(b + CH, hidden)) for b in range(0, hidden, CH)]

    depth = 16 * NX
    steps = SLOTS // depth

    def pre_copy(b):
        buf = lax.rem(b, 4)
        return pltpu.make_async_copy(pre.at[span(b * depth, depth, depth), :], pre_in.at[buf], p_sem.at[buf])

    def activations(b):
        pre_copy(b).wait()
        row = lax.broadcasted_iota(jnp.int32, (depth, depth), 0)
        column = lax.broadcasted_iota(jnp.int32, (depth, depth), 1)
        order = jnp.where(column == lax.rem(row, 16) * NX + row // 16, 1.0, 0.0).astype(BF)
        pre32[...] = nn(order, pre_in[lax.rem(b, 4)])

        @pl.when(b + 4 < steps)
        def _():
            pre_copy(b + 4).start()

        for xx in range(NX):
            src = slice(xx * 16, (xx + 1) * 16)
            gate, up = pre32[src, :hidden], pre32[src, hidden:]
            sig = 1.0 / (1.0 + jnp.exp(-gate))
            dst = span(xx * GRP + b * 16, 16, 16)
            g_gate[dst, :] = (up * sig * (1.0 + gate * (1.0 - sig))).astype(BF)
            g_up[dst, :] = (gate * sig).astype(BF)
            act = (gate * sig * up).astype(BF)
            for i, cols in enumerate(tiles):
                stage[i, dst, 0 : cols.stop - cols.start] = act[:, cols]

    for b in range(4):
        pre_copy(b).start()
    mine = span(z * BLK, BLK, BLK)
    meta[z] = jnp.full(meta.shape[1:], -1.0, F32)
    meta[z, 0:TOP, :] = ids[...].astype(F32)
    meta[z, 8 : 8 + TOP, :] = gates[...]
    weights[0, own] = w_down[...]
    w_start(0)
    weights[1, own] = w_gate[...]
    weights[2, own] = w_up[...]
    for b in range(len(tiles)):
        gh[b] = jnp.zeros((SLOTS, CH), F32)

    gather_at = 4 * LAG
    relay_at = gather_at + X_LAG
    ready_at = gather_at + 2 * X_LAG
    early = n // 2
    back_at = n + early
    late_at = back_at + n
    sums_at = back_at + ready_at

    def tick(t, carry):
        for s in (4, 3, 2, 1, 0):
            j = t - LAG * s

            @pl.when((j >= 0) & (j < 2 * n))
            def _():
                @pl.when(j == 0)
                def _():
                    for i in range(2):
                        if s > 0:
                            ring_meta(i, s - 1, s).wait_recv()
                        if s < 4:
                            ring_meta(i, s, s).start()

                if s == 0:
                    columns = span(block_of(lax.rem(j, n)) * CH, CH, CH)

                    @pl.when(j < n)
                    def _():
                        ag[lax.rem(j, AG_SLOTS), mine, :] = cot[:, columns]

                    @pl.when(j >= n)
                    def _():
                        ag[lax.rem(j, AG_SLOTS), mine, :] = tok[:, columns]

                for i in range(2):
                    if s > 0:
                        ring(i, j, s - 1, s).wait_recv()
                    if s < 4:
                        ring(i, j, s, s).start()

        for s in (4, 3, 2, 1):
            k = t - sums_at - SUM_LAG * s

            @pl.when((k >= 0) & (k < n))
            def _():
                if s == 4:
                    total = part[k, mine, :].astype(F32)
                    for i in range(2):
                        back_ring(i, k, 3).wait_recv()
                        total = total + z_in[i, k, 3].astype(F32)
                    out[:, span(block_of(k) * CH, CH, CH)] = total.astype(BF)
                else:
                    for i in range(2):
                        dest = lax.rem(z + z_step[i] * (4 - s), NZ)
                        back_ring(i, k, s - 1).wait_recv()
                        block = span(dest * BLK, BLK, BLK)
                        if s == 1:
                            first = (i * 4 + s) * BLK
                            for p in range(2):
                                value = part[k, span(dest * BLK + p * HALF, HALF, HALF), :]
                                if p == i:
                                    value = (value.astype(F32) + z_in[i, k, 0, 0:HALF, :].astype(F32)).astype(BF)
                                ag[AG_SLOTS - n + k, first + p * HALF : first + (p + 1) * HALF, :] = value
                        else:
                            value = part[k, block, :].astype(F32) + z_in[i, k, s - 1].astype(F32)
                            back_out(i, k, s)[...] = value.astype(BF)
                        back_ring(i, k, s).start()

        jr = t - relay_at

        @pl.when((jr >= 0) & (jr < 3 * n))
        def _():
            for i in range(2):
                x_arrival(jr, 2 + i).wait_recv()
                x_copy(jr, 4 + i).start()

        j = t - gather_at

        @pl.when(j == 0)
        def _():
            build_picker(z, meta, pick, slot_gate)

        @pl.when((j >= 0) & (j < 2 * n))
        def _():
            for i in range(2):
                for s in range(4):
                    ring(i, j, s, s).wait_send()

        @pl.when((j >= 4) & (j < 3 * n))
        def _():
            for what in range(4):
                x_copy(j - 4, what).wait_send()

        @pl.when(((j >= 0) & (j < back_at)) | ((j >= late_at) & (j < 3 * n)))
        def _():
            plain = (j >= n).astype(F32)
            chunk = j - n * (j // late_at)
            rows32[...] = nn(pick[...], ag[lax.rem(chunk, AG_SLOTS)]) * (slot_gate[...] * (1.0 - plain) + plain)

        @pl.when((j >= back_at) & (j < late_at))
        def _():
            block = block_of(j - back_at)
            rows32[...] = nn(g_gate[...], weights[1, block]) + nn(g_up[...], weights[2, block])

        @pl.when((j >= 0) & (j < 3 * n))
        def _():
            for d in (2, 1, 3, 0):
                rows = span(lax.rem(x + d, NX) * GRP, GRP, 16)
                if d == 0:
                    slot[lax.rem(j, 2 * n), rows, :] = rows32[rows, :].astype(BF)
                else:
                    stage[lax.rem(j, 4), rows, :] = rows32[rows, :].astype(BF)
                for what in {2: (2, 3), 1: (0,), 3: (1,), 0: ()}[d]:
                    x_copy(j, what).start()

        ja = t - ready_at

        @pl.when((ja >= 0) & (ja < 3 * n))
        def _():
            for what in (0, 1, 4, 5):
                x_arrival(ja, what).wait_recv()

        @pl.when((ja >= 1) & (ja < 3 * n + 1))
        def _():
            for what in (4, 5):
                x_copy(ja - 1, what).wait_send()

        for when, step in (
            (5, lambda: (w_forward(0), w_start(1))),
            (8, lambda: w_far(0)),
            (10, lambda: (w_forward(1), w_start(2))),
            (12, lambda: w_done(0)),
            (13, lambda: w_far(1)),
            (14, lambda: w_forward(2)),
            (16, lambda: (w_done(1), w_far(2))),
            (18, lambda: w_done(2)),
        ):

            @pl.when(t == when)
            def _():
                step()

        for b in range(2):

            @pl.when(t * 2 + b < steps)
            def _():
                activations(t * 2 + b)

        @pl.when(t == gather_at - 1)
        def _():
            for b, cols in enumerate(tiles):
                act_t[0, cols, :] = stage[b, :, 0 : cols.stop - cols.start].T

        @pl.when((j >= 1) & (j < 1 + NZ))
        def _():
            block = span((j - 1) * BLK, BLK, BLK)
            pick_t[block, :] = pick[:, block].T

        @pl.when((ja >= 0) & (ja < n))
        def _():
            block = block_of(ja)
            for b, cols in enumerate(tiles):
                gh[b, :, 0 : cols.stop - cols.start] += nt(slot[ja], weights[0, block, cols, :])

        @pl.when(ja == n - 1)
        def _():
            for b, cols in enumerate(tiles):
                grad = gh[b, :, 0 : cols.stop - cols.start]
                g_gate[:, cols] = (grad * g_gate[:, cols].astype(F32)).astype(BF)
                g_up[:, cols] = (grad * g_up[:, cols].astype(F32)).astype(BF)
            act_t[1] = g_gate[...].T
            act_t[2] = g_up[...].T

        @pl.when((ja >= 3) & (ja < n + 3))
        def _():
            reduce_block(0, ja - 3, ja - 3)

        @pl.when(((ja >= n) & (ja < back_at)) | ((ja >= late_at) & (ja < 3 * n)))
        def _():
            k = ja - n - n * (ja // late_at)
            reduce_block(1, k, lax.rem(ja, 2 * n))
            reduce_block(2, k, lax.rem(ja, 2 * n))

        @pl.when((ja >= back_at) & (ja < late_at))
        def _():
            k = ja - back_at
            part[k] = nn(pick_t[...], slot[lax.rem(ja, 2 * n)]).astype(BF)
            dest = lax.rem(z + 4, NZ)
            for i in range(2):
                back_out(i, k, 0)[...] = part[k, span(dest * BLK + i * HALF, HALF, HALF), :]
                back_ring(i, k, 0).start()

        return carry

    lax.fori_loop(0, max(sums_at + n + 4 * SUM_LAG, 3 * n + ready_at + 1), tick, 0)
    for i in range(2):
        for s in range(4):
            ring_meta(i, s, s).wait_send()

    def ended(k, carry):
        for i in range(2):
            for s in range(4):
                back_ring(i, k, s).wait_send()
        return carry

    lax.fori_loop(0, n, ended, 0)
    for j in range(3 * n - 4, 3 * n):
        for what in range(4):
            x_copy(j, what).wait_send()
    for m in range(3):
        for what in range(8):
            w_copy(m, what).wait_send()
        sib_copy(m, 3).wait_send()
        y_copy(m, 2).wait_send()
        y_copy(m, 3).wait_send()


def hand_out(rows, grads, out, grad_gate, grad_up, grad_down):
    out[...] = rows[...]
    for m, to in ((1, grad_gate), (2, grad_up), (0, grad_down)):
        to[...] = grads[m]


def shards(tokens, cotangent, expert_ids, gate_values, saved_pre, w_gate, w_up, w_down):
    width = tokens.shape[1]
    hidden = w_gate.shape[2]
    n = width // CH
    dma = pltpu.SemaphoreType.DMA
    vmem = pl.BlockSpec(memory_space=pltpu.VMEM)
    hbm = pl.BlockSpec(memory_space=pl.ANY)
    pre = saved_pre.reshape(NZ * NX, CAP, 2 * hidden).transpose(1, 0, 2).reshape(SLOTS, 2 * hidden)
    shape = jax.ShapeDtypeStruct
    rows, grads = pl.pallas_call(
        kernel,
        out_shape=(shape((BLK, width), BF), shape((3, hidden, CH), BF)),
        in_specs=[vmem] * 4 + [hbm] + [vmem] * 3,
        out_specs=(vmem, vmem),
        scratch_shapes=[
            pltpu.VMEM((NZ, 16, BLK), F32),
            pltpu.VMEM((AG_SLOTS, NZ * BLK, CH), BF),
            pltpu.VMEM((2 * n, SLOTS, CH), BF),
            pltpu.VMEM((4, SLOTS, CH), BF),
            pltpu.VMEM((n, GRP, CH), BF),
            pltpu.VMEM((SLOTS, NZ * BLK), BF),
            pltpu.VMEM((NZ * BLK, SLOTS), BF),
            pltpu.VMEM((SLOTS, 1), F32),
            pltpu.VMEM((n, NZ * BLK, CH), BF),
            pltpu.VMEM((2, n, 4, BLK, CH), BF),
            pltpu.VMEM((3, n, hidden, CH), BF),
            pltpu.VMEM((3, SLOTS, CH), F32),
            pltpu.VMEM((SLOTS, hidden), BF),
            pltpu.VMEM((SLOTS, hidden), BF),
            pltpu.VMEM((3, hidden, SLOTS), BF),
            pltpu.VMEM((4, 16 * NX, 2 * hidden), BF),
            pltpu.VMEM((16 * NX, 2 * hidden), F32),
            pltpu.VMEM((hidden, CH), F32),
            pltpu.VMEM((SLOTS, CH), F32),
            pltpu.VMEM((3, hidden, CH), BF),
            pltpu.VMEM((3, NY, hidden, CH), BF),
            pltpu.VMEM((3, 2, hidden, CH), BF),
            pltpu.VMEM((3, hidden, CH), BF),
            pltpu.VMEM((3, 2, hidden, CH), BF),
            dma((2, 2 * n, 4)),
            dma((2, 2 * n, 4)),
            dma((2, 4)),
            dma((2, 4)),
            dma((n, 6)),
            dma((n, 6)),
            dma((2, n, 4)),
            dma((2, n, 4)),
            dma((3, 8)),
            dma((3, 8)),
            dma((3, NY)),
            dma((3, NY)),
            dma((3, 4)),
            dma((3, 4)),
            dma((4,)),
        ],
        compiler_params=pltpu.CompilerParams(
            collective_id=0, has_side_effects=True, vmem_limit_bytes=62 * 2**20
        ),
        cost_estimate=pl.CostEstimate(flops=26 * 10**9, bytes_accessed=10 * 2**20, transcendentals=10**6),
        name="expert_backward",
    )(cotangent, tokens, expert_ids.T, gate_values.T, pre, w_gate[0].T, w_up[0].T, w_down[0])
    out, grad_gate, grad_up, grad_down = pl.pallas_call(
        hand_out,
        out_shape=(shape((BLK, width), BF), *[shape((hidden, CH), BF)] * 3),
        in_specs=[vmem] * 2,
        out_specs=(vmem,) * 4,
        name="hand_out",
    )(rows, grads)
    return (out, grad_gate.T[None], grad_up.T[None], grad_down[None])


def solution(mesh):
    tok = P(("dp", "expert"), None)
    row = P("expert", "dp", None)
    col = P("expert", None, "dp")
    return jax.shard_map(
        shards,
        mesh=mesh,
        in_specs=(tok, tok, tok, tok, P("expert", "dp", None, None, None), row, row, col),
        out_specs=(tok, row, row, col),
        check_vma=False,
    )
```

```python
import jax
import jax.numpy as jnp
from jax import lax
from jax.experimental import pallas as pl
from jax.experimental.pallas import tpu as pltpu
from jax.sharding import PartitionSpec as P

MESH = pl.DeviceIdType.MESH
NZ, NX, NY = 8, 4, 4
CAP = 26
TOP = 6
BLK = 128
GRP = NZ * CAP
SLOTS = NX * GRP
CH = 256
VIA = 112
LAG = 2
X_LAG = 1
SUM_LAG = 2
AG_SLOTS = 12
HALF = BLK // 2
BF = jnp.bfloat16
F32 = jnp.float32


def nt(a, b):
    return lax.dot_general(a, b, (((1,), (1,)), ((), ())), preferred_element_type=F32)


def tn(a, b):
    return lax.dot_general(a, b, (((0,), (0,)), ((), ())), preferred_element_type=F32)


def nn(a, b):
    return jnp.dot(a, b, preferred_element_type=F32)


def span(start, size, unit):
    return pl.ds(pl.multiple_of(start, unit), size)


def build_picker(z, meta, pick, slot_gate):
    ids = meta[:, 0:8, :]
    gates = meta[:, 8:16, :]
    upper = (
        lax.broadcasted_iota(jnp.int32, (BLK, BLK), 0) < lax.broadcasted_iota(jnp.int32, (BLK, BLK), 1)
    ).astype(BF)
    row = lax.broadcasted_iota(jnp.int32, (GRP, BLK), 0)
    base = lax.broadcasted_iota(jnp.int32, (NZ, BLK), 0)
    for xp in range(NX):
        same = ids == (z * NX + xp).astype(F32)
        named = jnp.sum(jnp.where(same, 1.0, 0.0), axis=1)
        gate = jnp.sum(jnp.where(same, gates, 0.0), axis=1)
        earlier = nn(named.astype(BF), upper).astype(jnp.int32)
        key = jnp.where(named > 0.5, base + earlier * NZ, -1)
        total = jnp.zeros((GRP, BLK), F32)
        for zz in range(NZ):
            hit = row == key[zz : zz + 1, :]
            pick[xp * GRP : (xp + 1) * GRP, zz * BLK : (zz + 1) * BLK] = jnp.where(hit, 1.0, 0.0).astype(BF)
            total = total + jnp.where(hit, gate[zz : zz + 1, :], 0.0)
        slot_gate[xp * GRP : (xp + 1) * GRP, :] = jnp.sum(total, axis=1, keepdims=True)


def kernel(
    cot, tok, ids, gates, pre, w_gate, w_up, w_down, out, grads,
    meta, ag, slot, stage, relay, pick, pick_t, slot_gate, part, z_in, weights, gh, g_gate, g_up, act_t,
    pre_in, pre32, tmp, rows32, sib_out, sib_in, y_out, y_half, y_full,
    z_send, z_recv, m_send, m_recv, x_send, x_recv, b_send, b_recv, w_send, w_recv, s_send, s_recv, y_send, y_recv, p_sem,
):
    r, e = lax.axis_index("dp"), lax.axis_index("expert")
    y, c = r // 2, lax.rem(r, 2)
    z, x = e // NX, lax.rem(e, NX)
    hidden = w_gate.shape[0]
    half_hid = hidden // 2
    n = cot.shape[1] // CH

    def at(yy=y, cc=c, zz=z, xx=x):
        return (yy * 2 + cc, zz * NX + xx)

    z_to = (at(zz=lax.rem(z + 1, NZ)), at(zz=lax.rem(z + NZ - 1, NZ)))
    x_to = (at(xx=lax.rem(x + 1, NX)), at(xx=lax.rem(x + NX - 1, NX)))
    y_to = (at(yy=lax.rem(y + 1, NY)), at(yy=lax.rem(y + NY - 1, NY)))
    sibling = at(cc=1 - c)
    z_step = (1, NZ - 1)
    low = lax.rem(y + NY - 1, NY)
    high = lax.rem(y + 1, NY)
    far_y = lax.rem(y + 2, NY)
    own = y * 2 + c
    upper_half, lower_half = slice(0, half_hid), slice(half_hid, hidden)
    barrier = pltpu.get_barrier_semaphore()
    peers = (*z_to, *x_to, *y_to, sibling)
    for peer in peers:
        pl.semaphore_signal(barrier, inc=1, device_id=peer, device_id_type=MESH)
    pl.semaphore_wait(barrier, len(peers))

    def send(src, dst, s_sem, r_sem, to):
        return pltpu.make_async_remote_copy(
            src_ref=src, dst_ref=dst, send_sem=s_sem, recv_sem=r_sem, device_id=to, device_id_type=MESH
        )

    def block_of(k):
        q = k // 2
        off = 2 - q + 3 * (q // 2) - 2 * (q // 3)
        core = c + (1 - 2 * c) * (1 - lax.rem(k, 2))
        return lax.rem(y + off, NY) * 2 + core

    def w_copy(m, what):
        view, to = (
            (weights.at[m, own], y_to[0]),
            (weights.at[m, own], y_to[1]),
            (weights.at[m, low * 2 + c, upper_half, :], y_to[0]),
            (weights.at[m, high * 2 + c, lower_half, :], y_to[1]),
            (weights.at[m, own], sibling),
            (weights.at[m, low * 2 + c], sibling),
            (weights.at[m, high * 2 + c], sibling),
            (weights.at[m, far_y * 2 + c], sibling),
        )[what]
        return send(view, view, w_send.at[m, what], w_recv.at[m, what], to)

    def w_arrival(m, what):
        view, source = (
            (weights.at[m, low * 2 + c], y_to[1]),
            (weights.at[m, high * 2 + c], y_to[0]),
            (weights.at[m, far_y * 2 + c, upper_half, :], y_to[1]),
            (weights.at[m, far_y * 2 + c, lower_half, :], y_to[0]),
            (weights.at[m, y * 2 + 1 - c], sibling),
            (weights.at[m, low * 2 + 1 - c], sibling),
            (weights.at[m, high * 2 + 1 - c], sibling),
            (weights.at[m, far_y * 2 + 1 - c], sibling),
        )[what]
        return send(view, view, w_send.at[m, what], w_recv.at[m, what], source)

    def w_start(m):
        for what in (0, 1, 4):
            w_copy(m, what).start()

    def w_forward(m):
        for i in range(2):
            w_arrival(m, i).wait_recv()
            w_copy(m, 2 + i).start()
            w_copy(m, 5 + i).start()

    def w_far(m):
        for i in range(2):
            w_arrival(m, 2 + i).wait_recv()
        w_copy(m, 7).start()

    def w_done(m):
        for what in range(4, 8):
            w_arrival(m, what).wait_recv()

    def ring(i, j, s, dist):
        origin = lax.rem(z + dist * (NZ - z_step[i]), NZ)
        rows = span(origin * BLK + i * HALF, HALF, HALF) if s == 3 else span(origin * BLK, BLK, BLK)
        view = ag.at[lax.rem(j, AG_SLOTS), rows, :]
        return send(view, view, z_send.at[i, j, s], z_recv.at[i, j, s], z_to[i])

    def ring_meta(i, s, dist):
        origin = lax.rem(z + dist * (NZ - z_step[i]), NZ)
        view = meta.at[origin, i * 8 : i * 8 + 8, :] if s == 3 else meta.at[origin]
        return send(view, view, m_send.at[i, s], m_recv.at[i, s], z_to[i])

    def x_copy(j, what):
        i = what % 2
        st, sl, rl = lax.rem(j, 4), lax.rem(j, 2 * n), lax.rem(j, n)
        near = lax.rem(x + (1 if i == 0 else NX - 1), NX) * GRP
        far = lax.rem(x + 2, NX) * GRP
        other = lax.rem(x + (NX - 1 if i == 0 else 1), NX) * GRP
        lo, size = (0, VIA) if i == 0 else (VIA, GRP - VIA)
        if what < 2:
            src, dst = stage.at[st, span(near, GRP, 16), :], slot.at[sl, span(x * GRP, GRP, 16), :]
        elif what < 4:
            src, dst = stage.at[st, span(far + lo, size, 16), :], relay.at[rl, lo : lo + size, :]
        else:
            src, dst = relay.at[rl, lo : lo + size, :], slot.at[sl, span(other + lo, size, 16), :]
        return send(src, dst, x_send.at[rl, what], x_recv.at[rl, what], x_to[i])

    def x_arrival(j, what):
        i = what % 2
        sl, rl = lax.rem(j, 2 * n), lax.rem(j, n)
        other = lax.rem(x + (NX - 1 if i == 0 else 1), NX) * GRP
        far = lax.rem(x + 2, NX) * GRP
        lo, size = (0, VIA) if i == 0 else (VIA, GRP - VIA)
        if what < 2:
            view = slot.at[sl, span(other, GRP, 16), :]
        elif what < 4:
            view = relay.at[rl, lo : lo + size, :]
        else:
            view = slot.at[sl, span(far + lo, size, 16), :]
        return send(view, view, x_send.at[rl, what], x_recv.at[rl, what], x_to[1 - i])

    def back_out(i, k, s):
        first = (i * 4 + s) * BLK
        return ag.at[AG_SLOTS - n + k, first : first + (HALF if s == 0 else BLK), :]

    def back_ring(i, k, s):
        dst = z_in.at[i, k, s, 0 : HALF if s == 0 else BLK, :]
        return send(back_out(i, k, s), dst, b_send.at[i, k, s], b_recv.at[i, k, s], z_to[i])

    def sib_copy(m, q):
        return send(sib_out.at[m], sib_in.at[m, q], s_send.at[m, q], s_recv.at[m, q], sibling)

    def y_copy(m, what):
        src, dst, to = (
            (y_out.at[m, 0, upper_half, :], y_half.at[m, upper_half, :], y_to[0]),
            (y_out.at[m, 0, lower_half, :], y_half.at[m, lower_half, :], y_to[1]),
            (y_out.at[m, 1], y_full.at[m, 0], y_to[0]),
            (y_out.at[m, 0], y_full.at[m, 1], y_to[1]),
        )[what]
        return send(src, dst, y_send.at[m, what], y_recv.at[m, what], to)

    def reduce_block(m, k, chunk):
        q = k // 2
        tmp[...] = nn(act_t[m], slot[chunk])

        @pl.when(lax.rem(k, 2) == 0)
        def _():
            @pl.when(q > 0)
            def _():
                sib_copy(m, q - 1).wait_send()

            sib_out[m] = tmp[...].astype(BF)
            sib_copy(m, q).start()

        @pl.when(lax.rem(k, 2) == 1)
        def _():
            sib_copy(m, q).wait_recv()
            tmp[...] += sib_in[m, q].astype(F32)

        @pl.when(k == 1)
        def _():
            y_out[m, 0] = tmp[...].astype(BF)
            y_copy(m, 0).start()
            y_copy(m, 1).start()

        @pl.when(k == 3)
        def _():
            y_copy(m, 0).wait_recv()
            tmp[upper_half, :] += y_half[m, upper_half, :].astype(F32)
            y_out[m, 1] = tmp[...].astype(BF)
            y_copy(m, 2).start()

        @pl.when(k == 5)
        def _():
            y_copy(m, 0).wait_send()
            y_copy(m, 1).wait_send()
            y_copy(m, 1).wait_recv()
            tmp[lower_half, :] += y_half[m, lower_half, :].astype(F32)
            y_out[m, 0] = tmp[...].astype(BF)
            y_copy(m, 3).start()

        @pl.when(k == 7)
        def _():
            y_copy(m, 2).wait_recv()
            y_copy(m, 3).wait_recv()
            grads[m] = (tmp[...] + y_full[m, 0].astype(F32) + y_full[m, 1].astype(F32)).astype(BF)

    tiles = [slice(b, min(b + CH, hidden)) for b in range(0, hidden, CH)]

    depth = 16 * NX
    steps = SLOTS // depth

    def pre_copy(b):
        buf = lax.rem(b, 4)
        return pltpu.make_async_copy(pre.at[span(b * depth, depth, depth), :], pre_in.at[buf], p_sem.at[buf])

    def activations(b):
        pre_copy(b).wait()
        row = lax.broadcasted_iota(jnp.int32, (depth, depth), 0)
        column = lax.broadcasted_iota(jnp.int32, (depth, depth), 1)
        order = jnp.where(column == lax.rem(row, 16) * NX + row // 16, 1.0, 0.0).astype(BF)
        pre32[...] = nn(order, pre_in[lax.rem(b, 4)])

        @pl.when(b + 4 < steps)
        def _():
            pre_copy(b + 4).start()

        for xx in range(NX):
            src = slice(xx * 16, (xx + 1) * 16)
            gate, up = pre32[src, :hidden], pre32[src, hidden:]
            sig = 1.0 / (1.0 + jnp.exp(-gate))
            dst = span(xx * GRP + b * 16, 16, 16)
            g_gate[dst, :] = (up * sig * (1.0 + gate * (1.0 - sig))).astype(BF)
            g_up[dst, :] = (gate * sig).astype(BF)
            act = (gate * sig * up).astype(BF)
            for i, cols in enumerate(tiles):
                stage[i, dst, 0 : cols.stop - cols.start] = act[:, cols]

    for b in range(4):
        pre_copy(b).start()
    mine = span(z * BLK, BLK, BLK)
    meta[z] = jnp.full(meta.shape[1:], -1.0, F32)
    meta[z, 0:TOP, :] = ids[...].astype(F32)
    meta[z, 8 : 8 + TOP, :] = gates[...]
    weights[0, own] = w_down[...]
    w_start(0)
    weights[1, own] = w_gate[...]
    weights[2, own] = w_up[...]
    for b in range(len(tiles)):
        gh[b] = jnp.zeros((SLOTS, CH), F32)

    gather_at = 4 * LAG
    per_tick = -(-steps // gather_at)
    relay_at = gather_at + X_LAG
    ready_at = gather_at + 2 * X_LAG
    early = n // 4
    back_at = n + early
    late_at = back_at + n
    sums_at = back_at + ready_at

    def tick(t, carry):
        for s in (4, 3, 2, 1, 0):
            j = t - LAG * s

            @pl.when((j >= 0) & (j < 2 * n))
            def _():
                @pl.when(j == 0)
                def _():
                    for i in range(2):
                        if s > 0:
                            ring_meta(i, s - 1, s).wait_recv()
                        if s < 4:
                            ring_meta(i, s, s).start()

                if s == 0:
                    columns = span(block_of(lax.rem(j, n)) * CH, CH, CH)

                    @pl.when(j < n)
                    def _():
                        ag[lax.rem(j, AG_SLOTS), mine, :] = cot[:, columns]

                    @pl.when(j >= n)
                    def _():
                        ag[lax.rem(j, AG_SLOTS), mine, :] = tok[:, columns]

                for i in range(2):
                    if s > 0:
                        ring(i, j, s - 1, s).wait_recv()
                    if s < 4:
                        ring(i, j, s, s).start()

        for s in (4, 3, 2, 1):
            k = t - sums_at - SUM_LAG * s

            @pl.when((k >= 0) & (k < n))
            def _():
                if s == 4:
                    total = part[k, mine, :].astype(F32)
                    for i in range(2):
                        back_ring(i, k, 3).wait_recv()
                        total = total + z_in[i, k, 3].astype(F32)
                    out[:, span(block_of(k) * CH, CH, CH)] = total.astype(BF)
                else:
                    for i in range(2):
                        dest = lax.rem(z + z_step[i] * (4 - s), NZ)
                        back_ring(i, k, s - 1).wait_recv()
                        block = span(dest * BLK, BLK, BLK)
                        if s == 1:
                            first = (i * 4 + s) * BLK
                            for p in range(2):
                                value = part[k, span(dest * BLK + p * HALF, HALF, HALF), :]
                                if p == i:
                                    value = (value.astype(F32) + z_in[i, k, 0, 0:HALF, :].astype(F32)).astype(BF)
                                ag[AG_SLOTS - n + k, first + p * HALF : first + (p + 1) * HALF, :] = value
                        else:
                            value = part[k, block, :].astype(F32) + z_in[i, k, s - 1].astype(F32)
                            back_out(i, k, s)[...] = value.astype(BF)
                        back_ring(i, k, s).start()

        jr = t - relay_at

        @pl.when((jr >= 0) & (jr < 3 * n))
        def _():
            for i in range(2):
                x_arrival(jr, 2 + i).wait_recv()
                x_copy(jr, 4 + i).start()

        j = t - gather_at

        @pl.when(j == 0)
        def _():
            build_picker(z, meta, pick, slot_gate)

        @pl.when((j >= 0) & (j < 2 * n))
        def _():
            for i in range(2):
                for s in range(4):
                    ring(i, j, s, s).wait_send()

        @pl.when((j >= 4) & (j < 3 * n))
        def _():
            for what in range(4):
                x_copy(j - 4, what).wait_send()

        @pl.when(((j >= 0) & (j < back_at)) | ((j >= late_at) & (j < 3 * n)))
        def _():
            plain = (j >= n).astype(F32)
            chunk = j - n * (j // late_at)
            rows32[...] = nn(pick[...], ag[lax.rem(chunk, AG_SLOTS)]) * (slot_gate[...] * (1.0 - plain) + plain)

        @pl.when((j >= back_at) & (j < late_at))
        def _():
            block = block_of(j - back_at)
            rows32[...] = nn(g_gate[...], weights[1, block]) + nn(g_up[...], weights[2, block])

        @pl.when((j >= 0) & (j < 3 * n))
        def _():
            for d in (2, 1, 3, 0):
                rows = span(lax.rem(x + d, NX) * GRP, GRP, 16)
                if d == 0:
                    slot[lax.rem(j, 2 * n), rows, :] = rows32[rows, :].astype(BF)
                else:
                    stage[lax.rem(j, 4), rows, :] = rows32[rows, :].astype(BF)
                for what in {2: (2, 3), 1: (0,), 3: (1,), 0: ()}[d]:
                    x_copy(j, what).start()

        ja = t - ready_at

        @pl.when((ja >= 0) & (ja < 3 * n))
        def _():
            for what in (0, 1, 4, 5):
                x_arrival(ja, what).wait_recv()

        @pl.when((ja >= 1) & (ja < 3 * n + 1))
        def _():
            for what in (4, 5):
                x_copy(ja - 1, what).wait_send()

        for when, step in (
            (3, lambda: (w_forward(0), w_start(1))),
            (5, lambda: w_far(0)),
            (6, lambda: (w_forward(1), w_start(2))),
            (ready_at, lambda: (w_done(0), w_far(1))),
            (ready_at + 1, lambda: w_forward(2)),
            (ready_at + 3, lambda: (w_done(1), w_far(2))),
            (ready_at + 5, lambda: w_done(2)),
        ):

            @pl.when(t == when)
            def _():
                step()

        for b in range(per_tick):

            @pl.when((t < gather_at) & (t * per_tick + b < steps))
            def _():
                activations(t * per_tick + b)

        @pl.when(t == gather_at - 1)
        def _():
            for b, cols in enumerate(tiles):
                act_t[0, cols, :] = stage[b, :, 0 : cols.stop - cols.start].T

        @pl.when((j >= 1) & (j < 1 + NZ))
        def _():
            block = span((j - 1) * BLK, BLK, BLK)
            pick_t[block, :] = pick[:, block].T

        @pl.when((ja >= 0) & (ja < n))
        def _():
            block = block_of(ja)
            for b, cols in enumerate(tiles):
                gh[b, :, 0 : cols.stop - cols.start] += nt(slot[ja], weights[0, block, cols, :])

        @pl.when(ja == n - 1)
        def _():
            for b, cols in enumerate(tiles):
                grad = gh[b, :, 0 : cols.stop - cols.start]
                g_gate[:, cols] = (grad * g_gate[:, cols].astype(F32)).astype(BF)
                g_up[:, cols] = (grad * g_up[:, cols].astype(F32)).astype(BF)
            act_t[1] = g_gate[...].T
            act_t[2] = g_up[...].T

        @pl.when((ja >= 3) & (ja < n + 3))
        def _():
            reduce_block(0, ja - 3, ja - 3)

        @pl.when(((ja >= n) & (ja < back_at)) | ((ja >= late_at) & (ja < 3 * n)))
        def _():
            k = ja - n - n * (ja // late_at)
            reduce_block(1, k, lax.rem(ja, 2 * n))
            reduce_block(2, k, lax.rem(ja, 2 * n))

        @pl.when((ja >= back_at) & (ja < late_at))
        def _():
            k = ja - back_at
            part[k] = nn(pick_t[...], slot[lax.rem(ja, 2 * n)]).astype(BF)
            dest = lax.rem(z + 4, NZ)
            for i in range(2):
                back_out(i, k, 0)[...] = part[k, span(dest * BLK + i * HALF, HALF, HALF), :]
                back_ring(i, k, 0).start()

        return carry

    lax.fori_loop(0, max(sums_at + n + 4 * SUM_LAG, 3 * n + ready_at + 1), tick, 0)
    for i in range(2):
        for s in range(4):
            ring_meta(i, s, s).wait_send()

    def ended(k, carry):
        for i in range(2):
            for s in range(4):
                back_ring(i, k, s).wait_send()
        return carry

    lax.fori_loop(0, n, ended, 0)
    for j in range(3 * n - 4, 3 * n):
        for what in range(4):
            x_copy(j, what).wait_send()
    for m in range(3):
        for what in range(8):
            w_copy(m, what).wait_send()
        sib_copy(m, 3).wait_send()
        y_copy(m, 2).wait_send()
        y_copy(m, 3).wait_send()


def hand_out(rows, grads, out, grad_gate, grad_up, grad_down):
    out[...] = rows[...]
    for m, to in ((1, grad_gate), (2, grad_up), (0, grad_down)):
        to[...] = grads[m]


def shards(tokens, cotangent, expert_ids, gate_values, saved_pre, w_gate, w_up, w_down):
    width = tokens.shape[1]
    hidden = w_gate.shape[2]
    n = width // CH
    dma = pltpu.SemaphoreType.DMA
    vmem = pl.BlockSpec(memory_space=pltpu.VMEM)
    hbm = pl.BlockSpec(memory_space=pl.ANY)
    pre = saved_pre.reshape(NZ * NX, CAP, 2 * hidden).transpose(1, 0, 2).reshape(SLOTS, 2 * hidden)
    shape = jax.ShapeDtypeStruct
    rows, grads = pl.pallas_call(
        kernel,
        out_shape=(shape((BLK, width), BF), shape((3, hidden, CH), BF)),
        in_specs=[vmem] * 4 + [hbm] + [vmem] * 3,
        out_specs=(vmem, vmem),
        scratch_shapes=[
            pltpu.VMEM((NZ, 16, BLK), F32),
            pltpu.VMEM((AG_SLOTS, NZ * BLK, CH), BF),
            pltpu.VMEM((2 * n, SLOTS, CH), BF),
            pltpu.VMEM((4, SLOTS, CH), BF),
            pltpu.VMEM((n, GRP, CH), BF),
            pltpu.VMEM((SLOTS, NZ * BLK), BF),
            pltpu.VMEM((NZ * BLK, SLOTS), BF),
            pltpu.VMEM((SLOTS, 1), F32),
            pltpu.VMEM((n, NZ * BLK, CH), BF),
            pltpu.VMEM((2, n, 4, BLK, CH), BF),
            pltpu.VMEM((3, n, hidden, CH), BF),
            pltpu.VMEM((3, SLOTS, CH), F32),
            pltpu.VMEM((SLOTS, hidden), BF),
            pltpu.VMEM((SLOTS, hidden), BF),
            pltpu.VMEM((3, hidden, SLOTS), BF),
            pltpu.VMEM((4, 16 * NX, 2 * hidden), BF),
            pltpu.VMEM((16 * NX, 2 * hidden), F32),
            pltpu.VMEM((hidden, CH), F32),
            pltpu.VMEM((SLOTS, CH), F32),
            pltpu.VMEM((3, hidden, CH), BF),
            pltpu.VMEM((3, NY, hidden, CH), BF),
            pltpu.VMEM((3, 2, hidden, CH), BF),
            pltpu.VMEM((3, hidden, CH), BF),
            pltpu.VMEM((3, 2, hidden, CH), BF),
            dma((2, 2 * n, 4)),
            dma((2, 2 * n, 4)),
            dma((2, 4)),
            dma((2, 4)),
            dma((n, 6)),
            dma((n, 6)),
            dma((2, n, 4)),
            dma((2, n, 4)),
            dma((3, 8)),
            dma((3, 8)),
            dma((3, NY)),
            dma((3, NY)),
            dma((3, 4)),
            dma((3, 4)),
            dma((4,)),
        ],
        compiler_params=pltpu.CompilerParams(
            collective_id=0, has_side_effects=True, vmem_limit_bytes=62 * 2**20
        ),
        cost_estimate=pl.CostEstimate(flops=26 * 10**9, bytes_accessed=10 * 2**20, transcendentals=10**6),
        name="expert_backward",
    )(cotangent, tokens, expert_ids.T, gate_values.T, pre, w_gate[0].T, w_up[0].T, w_down[0])
    out, grad_gate, grad_up, grad_down = pl.pallas_call(
        hand_out,
        out_shape=(shape((BLK, width), BF), *[shape((hidden, CH), BF)] * 3),
        in_specs=[vmem] * 2,
        out_specs=(vmem,) * 4,
        name="hand_out",
    )(rows, grads)
    return (out, grad_gate.T[None], grad_up.T[None], grad_down[None])


def solution(mesh):
    tok = P(("dp", "expert"), None)
    row = P("expert", "dp", None)
    col = P("expert", None, "dp")
    return jax.shard_map(
        shards,
        mesh=mesh,
        in_specs=(tok, tok, tok, tok, P("expert", "dp", None, None, None), row, row, col),
        out_specs=(tok, row, row, col),
        check_vma=False,
    )
```

```python
import jax
import jax.numpy as jnp
from jax import lax
from jax.experimental import pallas as pl
from jax.experimental.pallas import tpu as pltpu
from jax.sharding import PartitionSpec as P

MESH = pl.DeviceIdType.MESH
NZ, NX, NY = 8, 4, 4
CAP = 26
TOP = 6
BLK = 128
GRP = NZ * CAP
SLOTS = NX * GRP
CH = 256
VIA = 112
LAG = 2
X_LAG = 1
SUM_LAG = 2
AG_SLOTS = 12
HALF = BLK // 2
BF = jnp.bfloat16
F32 = jnp.float32


def nt(a, b):
    return lax.dot_general(a, b, (((1,), (1,)), ((), ())), preferred_element_type=F32)


def tn(a, b):
    return lax.dot_general(a, b, (((0,), (0,)), ((), ())), preferred_element_type=F32)


def nn(a, b):
    return jnp.dot(a, b, preferred_element_type=F32)


def span(start, size, unit):
    return pl.ds(pl.multiple_of(start, unit), size)


def build_picker(z, meta, pick, slot_gate):
    ids = meta[:, 0:8, :]
    gates = meta[:, 8:16, :]
    upper = (
        lax.broadcasted_iota(jnp.int32, (BLK, BLK), 0) < lax.broadcasted_iota(jnp.int32, (BLK, BLK), 1)
    ).astype(BF)
    row = lax.broadcasted_iota(jnp.int32, (GRP, BLK), 0)
    base = lax.broadcasted_iota(jnp.int32, (NZ, BLK), 0)
    for xp in range(NX):
        same = ids == (z * NX + xp).astype(F32)
        named = jnp.sum(jnp.where(same, 1.0, 0.0), axis=1)
        gate = jnp.sum(jnp.where(same, gates, 0.0), axis=1)
        earlier = nn(named.astype(BF), upper).astype(jnp.int32)
        key = jnp.where(named > 0.5, base + earlier * NZ, -1)
        total = jnp.zeros((GRP, BLK), F32)
        for zz in range(NZ):
            hit = row == key[zz : zz + 1, :]
            pick[xp * GRP : (xp + 1) * GRP, zz * BLK : (zz + 1) * BLK] = jnp.where(hit, 1.0, 0.0).astype(BF)
            total = total + jnp.where(hit, gate[zz : zz + 1, :], 0.0)
        slot_gate[xp * GRP : (xp + 1) * GRP, :] = jnp.sum(total, axis=1, keepdims=True)


def kernel(
    cot, tok, ids, gates, pre, w_gate, w_up, w_down, out, grads,
    meta, ag, slot, stage, relay, pick, pick_t, slot_gate, part, z_in, weights, gh, g_gate, g_up, act_t,
    pre_in, pre32, tmp, rows32, sib_out, sib_in, y_out, y_half, y_full,
    z_send, z_recv, m_send, m_recv, x_send, x_recv, b_send, b_recv, w_send, w_recv, s_send, s_recv, y_send, y_recv, p_sem,
):
    r, e = lax.axis_index("dp"), lax.axis_index("expert")
    y, c = r // 2, lax.rem(r, 2)
    z, x = e // NX, lax.rem(e, NX)
    hidden = w_gate.shape[0]
    half_hid = hidden // 2
    n = cot.shape[1] // CH

    def at(yy=y, cc=c, zz=z, xx=x):
        return (yy * 2 + cc, zz * NX + xx)

    z_to = (at(zz=lax.rem(z + 1, NZ)), at(zz=lax.rem(z + NZ - 1, NZ)))
    x_to = (at(xx=lax.rem(x + 1, NX)), at(xx=lax.rem(x + NX - 1, NX)))
    y_to = (at(yy=lax.rem(y + 1, NY)), at(yy=lax.rem(y + NY - 1, NY)))
    sibling = at(cc=1 - c)
    z_step = (1, NZ - 1)
    low = lax.rem(y + NY - 1, NY)
    high = lax.rem(y + 1, NY)
    far_y = lax.rem(y + 2, NY)
    own = y * 2 + c
    upper_half, lower_half = slice(0, half_hid), slice(half_hid, hidden)
    barrier = pltpu.get_barrier_semaphore()
    peers = (*z_to, *x_to, *y_to, sibling)
    for peer in peers:
        pl.semaphore_signal(barrier, inc=1, device_id=peer, device_id_type=MESH)
    pl.semaphore_wait(barrier, len(peers))

    def send(src, dst, s_sem, r_sem, to):
        return pltpu.make_async_remote_copy(
            src_ref=src, dst_ref=dst, send_sem=s_sem, recv_sem=r_sem, device_id=to, device_id_type=MESH
        )

    def block_of(k):
        q = k // 2
        off = 2 - q + 3 * (q // 2) - 2 * (q // 3)
        core = c + (1 - 2 * c) * (1 - lax.rem(k, 2))
        return lax.rem(y + off, NY) * 2 + core

    def w_copy(m, what):
        view, to = (
            (weights.at[m, own], y_to[0]),
            (weights.at[m, own], y_to[1]),
            (weights.at[m, low * 2 + c, upper_half, :], y_to[0]),
            (weights.at[m, high * 2 + c, lower_half, :], y_to[1]),
            (weights.at[m, own], sibling),
            (weights.at[m, low * 2 + c], sibling),
            (weights.at[m, high * 2 + c], sibling),
            (weights.at[m, far_y * 2 + c], sibling),
        )[what]
        return send(view, view, w_send.at[m, what], w_recv.at[m, what], to)

    def w_arrival(m, what):
        view, source = (
            (weights.at[m, low * 2 + c], y_to[1]),
            (weights.at[m, high * 2 + c], y_to[0]),
            (weights.at[m, far_y * 2 + c, upper_half, :], y_to[1]),
            (weights.at[m, far_y * 2 + c, lower_half, :], y_to[0]),
            (weights.at[m, y * 2 + 1 - c], sibling),
            (weights.at[m, low * 2 + 1 - c], sibling),
            (weights.at[m, high * 2 + 1 - c], sibling),
            (weights.at[m, far_y * 2 + 1 - c], sibling),
        )[what]
        return send(view, view, w_send.at[m, what], w_recv.at[m, what], source)

    def w_start(m):
        for what in (0, 1, 4):
            w_copy(m, what).start()

    def w_forward(m):
        for i in range(2):
            w_arrival(m, i).wait_recv()
            w_copy(m, 2 + i).start()
            w_copy(m, 5 + i).start()

    def w_far(m):
        for i in range(2):
            w_arrival(m, 2 + i).wait_recv()
        w_copy(m, 7).start()

    def w_done(m):
        for what in range(4, 8):
            w_arrival(m, what).wait_recv()

    def ring(i, j, s, dist):
        origin = lax.rem(z + dist * (NZ - z_step[i]), NZ)
        rows = span(origin * BLK + i * HALF, HALF, HALF) if s == 3 else span(origin * BLK, BLK, BLK)
        view = ag.at[lax.rem(j, AG_SLOTS), rows, :]
        return send(view, view, z_send.at[i, j, s], z_recv.at[i, j, s], z_to[i])

    def ring_meta(i, s, dist):
        origin = lax.rem(z + dist * (NZ - z_step[i]), NZ)
        view = meta.at[origin, i * 8 : i * 8 + 8, :] if s == 3 else meta.at[origin]
        return send(view, view, m_send.at[i, s], m_recv.at[i, s], z_to[i])

    def x_copy(j, what):
        i = what % 2
        st, sl, rl = lax.rem(j, 4), lax.rem(j, 2 * n), lax.rem(j, n)
        near = lax.rem(x + (1 if i == 0 else NX - 1), NX) * GRP
        far = lax.rem(x + 2, NX) * GRP
        other = lax.rem(x + (NX - 1 if i == 0 else 1), NX) * GRP
        lo, size = (0, VIA) if i == 0 else (VIA, GRP - VIA)
        if what < 2:
            src, dst = stage.at[st, span(near, GRP, 16), :], slot.at[sl, span(x * GRP, GRP, 16), :]
        elif what < 4:
            src, dst = stage.at[st, span(far + lo, size, 16), :], relay.at[rl, lo : lo + size, :]
        else:
            src, dst = relay.at[rl, lo : lo + size, :], slot.at[sl, span(other + lo, size, 16), :]
        return send(src, dst, x_send.at[rl, what], x_recv.at[rl, what], x_to[i])

    def x_arrival(j, what):
        i = what % 2
        sl, rl = lax.rem(j, 2 * n), lax.rem(j, n)
        other = lax.rem(x + (NX - 1 if i == 0 else 1), NX) * GRP
        far = lax.rem(x + 2, NX) * GRP
        lo, size = (0, VIA) if i == 0 else (VIA, GRP - VIA)
        if what < 2:
            view = slot.at[sl, span(other, GRP, 16), :]
        elif what < 4:
            view = relay.at[rl, lo : lo + size, :]
        else:
            view = slot.at[sl, span(far + lo, size, 16), :]
        return send(view, view, x_send.at[rl, what], x_recv.at[rl, what], x_to[1 - i])

    def back_out(i, k, s):
        first = (i * 4 + s) * BLK
        return ag.at[AG_SLOTS - n + k, first : first + (HALF if s == 0 else BLK), :]

    def back_ring(i, k, s):
        dst = z_in.at[i, k, s, 0 : HALF if s == 0 else BLK, :]
        return send(back_out(i, k, s), dst, b_send.at[i, k, s], b_recv.at[i, k, s], z_to[i])

    def sib_copy(m, q):
        return send(sib_out.at[m], sib_in.at[m, q], s_send.at[m, q], s_recv.at[m, q], sibling)

    def y_copy(m, what):
        src, dst, to = (
            (y_out.at[m, 0, upper_half, :], y_half.at[m, upper_half, :], y_to[0]),
            (y_out.at[m, 0, lower_half, :], y_half.at[m, lower_half, :], y_to[1]),
            (y_out.at[m, 1], y_full.at[m, 0], y_to[0]),
            (y_out.at[m, 0], y_full.at[m, 1], y_to[1]),
        )[what]
        return send(src, dst, y_send.at[m, what], y_recv.at[m, what], to)

    def reduce_block(m, k, chunk):
        q = k // 2
        tmp[...] = nn(act_t[m], slot[chunk])

        @pl.when(lax.rem(k, 2) == 0)
        def _():
            @pl.when(q > 0)
            def _():
                sib_copy(m, q - 1).wait_send()

            sib_out[m] = tmp[...].astype(BF)
            sib_copy(m, q).start()

        @pl.when(lax.rem(k, 2) == 1)
        def _():
            sib_copy(m, q).wait_recv()
            tmp[...] += sib_in[m, q].astype(F32)

        @pl.when(k == 1)
        def _():
            y_out[m, 0] = tmp[...].astype(BF)
            y_copy(m, 0).start()
            y_copy(m, 1).start()

        @pl.when(k == 3)
        def _():
            y_copy(m, 0).wait_recv()
            tmp[upper_half, :] += y_half[m, upper_half, :].astype(F32)
            y_out[m, 1] = tmp[...].astype(BF)
            y_copy(m, 2).start()

        @pl.when(k == 5)
        def _():
            y_copy(m, 0).wait_send()
            y_copy(m, 1).wait_send()
            y_copy(m, 1).wait_recv()
            tmp[lower_half, :] += y_half[m, lower_half, :].astype(F32)
            y_out[m, 0] = tmp[...].astype(BF)
            y_copy(m, 3).start()

        @pl.when(k == 7)
        def _():
            y_copy(m, 2).wait_recv()
            y_copy(m, 3).wait_recv()
            grads[m] = (tmp[...] + y_full[m, 0].astype(F32) + y_full[m, 1].astype(F32)).astype(BF)

    tiles = [slice(b, min(b + CH, hidden)) for b in range(0, hidden, CH)]

    depth = 16 * NX
    steps = SLOTS // depth

    def pre_copy(b):
        buf = lax.rem(b, 4)
        return pltpu.make_async_copy(pre.at[span(b * depth, depth, depth), :], pre_in.at[buf], p_sem.at[buf])

    def activations(b):
        pre_copy(b).wait()
        row = lax.broadcasted_iota(jnp.int32, (depth, depth), 0)
        column = lax.broadcasted_iota(jnp.int32, (depth, depth), 1)
        order = jnp.where(column == lax.rem(row, 16) * NX + row // 16, 1.0, 0.0).astype(BF)
        pre32[...] = nn(order, pre_in[lax.rem(b, 4)])

        @pl.when(b + 4 < steps)
        def _():
            pre_copy(b + 4).start()

        for xx in range(NX):
            src = slice(xx * 16, (xx + 1) * 16)
            gate, up = pre32[src, :hidden], pre32[src, hidden:]
            sig = 1.0 / (1.0 + jnp.exp(-gate))
            dst = span(xx * GRP + b * 16, 16, 16)
            g_gate[dst, :] = (up * sig * (1.0 + gate * (1.0 - sig))).astype(BF)
            g_up[dst, :] = (gate * sig).astype(BF)
            act = (gate * sig * up).astype(BF)
            for i, cols in enumerate(tiles):
                stage[i, dst, 0 : cols.stop - cols.start] = act[:, cols]

    for b in range(4):
        pre_copy(b).start()
    mine = span(z * BLK, BLK, BLK)
    meta[z] = jnp.full(meta.shape[1:], -1.0, F32)
    meta[z, 0:TOP, :] = ids[...].astype(F32)
    meta[z, 8 : 8 + TOP, :] = gates[...]
    weights[0, own] = w_down[...]
    w_start(0)
    weights[1, own] = w_gate[...]
    weights[2, own] = w_up[...]
    for b in range(len(tiles)):
        gh[b] = jnp.zeros((SLOTS, CH), F32)

    gather_at = 4 * LAG
    per_tick = -(-steps // gather_at)
    relay_at = gather_at + X_LAG
    ready_at = gather_at + 2 * X_LAG
    early = n // 4
    back_at = n + early
    late_at = back_at + n
    sums_at = back_at + ready_at

    def tick(t, carry):
        jr = t - relay_at

        @pl.when((jr >= 0) & (jr < 3 * n))
        def _():
            for i in range(2):
                x_arrival(jr, 2 + i).wait_recv()
                x_copy(jr, 4 + i).start()

        for s in (4, 3, 2, 1, 0):
            j = t - LAG * s

            @pl.when((j >= 0) & (j < 2 * n))
            def _():
                @pl.when(j == 0)
                def _():
                    for i in range(2):
                        if s > 0:
                            ring_meta(i, s - 1, s).wait_recv()
                        if s < 4:
                            ring_meta(i, s, s).start()

                if s == 0:
                    columns = span(block_of(lax.rem(j, n)) * CH, CH, CH)

                    @pl.when(j < n)
                    def _():
                        ag[lax.rem(j, AG_SLOTS), mine, :] = cot[:, columns]

                    @pl.when(j >= n)
                    def _():
                        ag[lax.rem(j, AG_SLOTS), mine, :] = tok[:, columns]

                for i in range(2):
                    if s > 0:
                        ring(i, j, s - 1, s).wait_recv()
                    if s < 4:
                        ring(i, j, s, s).start()

        for s in (4, 3, 2, 1):
            k = t - sums_at - SUM_LAG * s

            @pl.when((k >= 0) & (k < n))
            def _():
                if s == 4:
                    total = part[k, mine, :].astype(F32)
                    for i in range(2):
                        back_ring(i, k, 3).wait_recv()
                        total = total + z_in[i, k, 3].astype(F32)
                    out[:, span(block_of(k) * CH, CH, CH)] = total.astype(BF)
                else:
                    for i in range(2):
                        dest = lax.rem(z + z_step[i] * (4 - s), NZ)
                        back_ring(i, k, s - 1).wait_recv()
                        block = span(dest * BLK, BLK, BLK)
                        if s == 1:
                            first = (i * 4 + s) * BLK
                            for p in range(2):
                                value = part[k, span(dest * BLK + p * HALF, HALF, HALF), :]
                                if p == i:
                                    value = (value.astype(F32) + z_in[i, k, 0, 0:HALF, :].astype(F32)).astype(BF)
                                ag[AG_SLOTS - n + k, first + p * HALF : first + (p + 1) * HALF, :] = value
                        else:
                            value = part[k, block, :].astype(F32) + z_in[i, k, s - 1].astype(F32)
                            back_out(i, k, s)[...] = value.astype(BF)
                        back_ring(i, k, s).start()

        j = t - gather_at

        @pl.when(j == 0)
        def _():
            build_picker(z, meta, pick, slot_gate)

        @pl.when((j >= 0) & (j < 2 * n))
        def _():
            for i in range(2):
                for s in range(4):
                    ring(i, j, s, s).wait_send()

        @pl.when((j >= 4) & (j < 3 * n))
        def _():
            for what in range(4):
                x_copy(j - 4, what).wait_send()

        @pl.when(((j >= 0) & (j < back_at)) | ((j >= late_at) & (j < 3 * n)))
        def _():
            plain = (j >= n).astype(F32)
            chunk = j - n * (j // late_at)
            rows32[...] = nn(pick[...], ag[lax.rem(chunk, AG_SLOTS)]) * (slot_gate[...] * (1.0 - plain) + plain)

        @pl.when((j >= back_at) & (j < late_at))
        def _():
            block = block_of(j - back_at)
            rows32[...] = nn(g_gate[...], weights[1, block]) + nn(g_up[...], weights[2, block])

        @pl.when((j >= 0) & (j < 3 * n))
        def _():
            for d in (2, 1, 3, 0):
                rows = span(lax.rem(x + d, NX) * GRP, GRP, 16)
                if d == 0:
                    slot[lax.rem(j, 2 * n), rows, :] = rows32[rows, :].astype(BF)
                else:
                    stage[lax.rem(j, 4), rows, :] = rows32[rows, :].astype(BF)
                for what in {2: (2, 3), 1: (0,), 3: (1,), 0: ()}[d]:
                    x_copy(j, what).start()

        ja = t - ready_at

        @pl.when((ja >= 0) & (ja < 3 * n))
        def _():
            for what in (0, 1, 4, 5):
                x_arrival(ja, what).wait_recv()

        @pl.when((ja >= 1) & (ja < 3 * n + 1))
        def _():
            for what in (4, 5):
                x_copy(ja - 1, what).wait_send()

        for when, step in (
            (3, lambda: (w_forward(0), w_start(1))),
            (5, lambda: w_far(0)),
            (6, lambda: (w_forward(1), w_start(2))),
            (ready_at, lambda: (w_done(0), w_far(1))),
            (ready_at + 1, lambda: w_forward(2)),
            (ready_at + 3, lambda: (w_done(1), w_far(2))),
            (ready_at + 5, lambda: w_done(2)),
        ):

            @pl.when(t == when)
            def _():
                step()

        for b in range(per_tick):

            @pl.when((t < gather_at) & (t * per_tick + b < steps))
            def _():
                activations(t * per_tick + b)

        @pl.when(t == gather_at - 1)
        def _():
            for b, cols in enumerate(tiles):
                act_t[0, cols, :] = stage[b, :, 0 : cols.stop - cols.start].T

        @pl.when((j >= 1) & (j < 1 + NZ))
        def _():
            block = span((j - 1) * BLK, BLK, BLK)
            pick_t[block, :] = pick[:, block].T

        @pl.when((ja >= 0) & (ja < n))
        def _():
            block = block_of(ja)
            for b, cols in enumerate(tiles):
                gh[b, :, 0 : cols.stop - cols.start] += nt(slot[ja], weights[0, block, cols, :])

        @pl.when(ja == n - 1)
        def _():
            for b, cols in enumerate(tiles):
                grad = gh[b, :, 0 : cols.stop - cols.start]
                g_gate[:, cols] = (grad * g_gate[:, cols].astype(F32)).astype(BF)
                g_up[:, cols] = (grad * g_up[:, cols].astype(F32)).astype(BF)
            act_t[1] = g_gate[...].T
            act_t[2] = g_up[...].T

        @pl.when((ja >= 3) & (ja < n + 3))
        def _():
            reduce_block(0, ja - 3, ja - 3)

        @pl.when(((ja >= n) & (ja < back_at)) | ((ja >= late_at) & (ja < 3 * n)))
        def _():
            k = ja - n - n * (ja // late_at)
            reduce_block(1, k, lax.rem(ja, 2 * n))
            reduce_block(2, k, lax.rem(ja, 2 * n))

        @pl.when((ja >= back_at) & (ja < late_at))
        def _():
            k = ja - back_at
            part[k] = nn(pick_t[...], slot[lax.rem(ja, 2 * n)]).astype(BF)
            dest = lax.rem(z + 4, NZ)
            for i in range(2):
                back_out(i, k, 0)[...] = part[k, span(dest * BLK + i * HALF, HALF, HALF), :]
                back_ring(i, k, 0).start()

        return carry

    lax.fori_loop(0, max(sums_at + n + 4 * SUM_LAG, 3 * n + ready_at + 1), tick, 0)
    for i in range(2):
        for s in range(4):
            ring_meta(i, s, s).wait_send()

    def ended(k, carry):
        for i in range(2):
            for s in range(4):
                back_ring(i, k, s).wait_send()
        return carry

    lax.fori_loop(0, n, ended, 0)
    for j in range(3 * n - 4, 3 * n):
        for what in range(4):
            x_copy(j, what).wait_send()
    for m in range(3):
        for what in range(8):
            w_copy(m, what).wait_send()
        sib_copy(m, 3).wait_send()
        y_copy(m, 2).wait_send()
        y_copy(m, 3).wait_send()


def hand_out(rows, grads, out, grad_gate, grad_up, grad_down):
    out[...] = rows[...]
    for m, to in ((1, grad_gate), (2, grad_up), (0, grad_down)):
        to[...] = grads[m]


def shards(tokens, cotangent, expert_ids, gate_values, saved_pre, w_gate, w_up, w_down):
    width = tokens.shape[1]
    hidden = w_gate.shape[2]
    n = width // CH
    dma = pltpu.SemaphoreType.DMA
    vmem = pl.BlockSpec(memory_space=pltpu.VMEM)
    hbm = pl.BlockSpec(memory_space=pl.ANY)
    pre = saved_pre.reshape(NZ * NX, CAP, 2 * hidden).transpose(1, 0, 2).reshape(SLOTS, 2 * hidden)
    shape = jax.ShapeDtypeStruct
    rows, grads = pl.pallas_call(
        kernel,
        out_shape=(shape((BLK, width), BF), shape((3, hidden, CH), BF)),
        in_specs=[vmem] * 4 + [hbm] + [vmem] * 3,
        out_specs=(vmem, vmem),
        scratch_shapes=[
            pltpu.VMEM((NZ, 16, BLK), F32),
            pltpu.VMEM((AG_SLOTS, NZ * BLK, CH), BF),
            pltpu.VMEM((2 * n, SLOTS, CH), BF),
            pltpu.VMEM((4, SLOTS, CH), BF),
            pltpu.VMEM((n, GRP, CH), BF),
            pltpu.VMEM((SLOTS, NZ * BLK), BF),
            pltpu.VMEM((NZ * BLK, SLOTS), BF),
            pltpu.VMEM((SLOTS, 1), F32),
            pltpu.VMEM((n, NZ * BLK, CH), BF),
            pltpu.VMEM((2, n, 4, BLK, CH), BF),
            pltpu.VMEM((3, n, hidden, CH), BF),
            pltpu.VMEM((3, SLOTS, CH), F32),
            pltpu.VMEM((SLOTS, hidden), BF),
            pltpu.VMEM((SLOTS, hidden), BF),
            pltpu.VMEM((3, hidden, SLOTS), BF),
            pltpu.VMEM((4, 16 * NX, 2 * hidden), BF),
            pltpu.VMEM((16 * NX, 2 * hidden), F32),
            pltpu.VMEM((hidden, CH), F32),
            pltpu.VMEM((SLOTS, CH), F32),
            pltpu.VMEM((3, hidden, CH), BF),
            pltpu.VMEM((3, NY, hidden, CH), BF),
            pltpu.VMEM((3, 2, hidden, CH), BF),
            pltpu.VMEM((3, hidden, CH), BF),
            pltpu.VMEM((3, 2, hidden, CH), BF),
            dma((2, 2 * n, 4)),
            dma((2, 2 * n, 4)),
            dma((2, 4)),
            dma((2, 4)),
            dma((n, 6)),
            dma((n, 6)),
            dma((2, n, 4)),
            dma((2, n, 4)),
            dma((3, 8)),
            dma((3, 8)),
            dma((3, NY)),
            dma((3, NY)),
            dma((3, 4)),
            dma((3, 4)),
            dma((4,)),
        ],
        compiler_params=pltpu.CompilerParams(
            collective_id=0, has_side_effects=True, vmem_limit_bytes=62 * 2**20
        ),
        cost_estimate=pl.CostEstimate(flops=26 * 10**9, bytes_accessed=10 * 2**20, transcendentals=10**6),
        name="expert_backward",
    )(cotangent, tokens, expert_ids.T, gate_values.T, pre, w_gate[0].T, w_up[0].T, w_down[0])
    out, grad_gate, grad_up, grad_down = pl.pallas_call(
        hand_out,
        out_shape=(shape((BLK, width), BF), *[shape((hidden, CH), BF)] * 3),
        in_specs=[vmem] * 2,
        out_specs=(vmem,) * 4,
        name="hand_out",
    )(rows, grads)
    return (out, grad_gate.T[None], grad_up.T[None], grad_down[None])


def solution(mesh):
    tok = P(("dp", "expert"), None)
    row = P("expert", "dp", None)
    col = P("expert", None, "dp")
    return jax.shard_map(
        shards,
        mesh=mesh,
        in_specs=(tok, tok, tok, tok, P("expert", "dp", None, None, None), row, row, col),
        out_specs=(tok, row, row, col),
        check_vma=False,
    )
```
